128 devices in a mesh: spec: 2 (over y_lo), slab: 64 (over x, y_hi, z, core).
Axes of the slice: x: 4, y: 4 (y_hi: 2, y_lo: 2; y = y_hi * 2 + y_lo), z: 4, core: 2. Of those that a mesh axis runs over, the one named last changes fastest.
Arguments:
- amplitude: bfloat16 [512, 512, 256], P('slab'), may hold values from 0.5 to 1.5
- displacement: bfloat16 [3, 512, 512, 256], P(None, 'slab'), may hold values from -4 to 4
- support: int32 [512, 512, 256], P('slab'), may hold values 0 or 1
- counts: int32 [512, 512, 128], P(None, 'slab'), may hold values from 0 to 11
- bin_weights: float32 [4], replicated, may hold values from 0.5 to 2
- bin_scales: float32 [4], replicated, may hold values from 0.96 to 1.04
- bragg_vector: float32 [3], replicated, may hold values from 1 to 3
Outputs:
- new_amplitude: float32 [512, 512, 256], P('slab')
- new_displacement: bfloat16 [3, 512, 512, 256], P(None, 'slab')
The draws below stay inside these ranges and needn't reach their ends.
All inputs are finite; a program needn't handle non-finite values. No bound on the sum of `support` on one device may be relied on, other than what follows from the above.
Results may differ from the reference program's by a relative error of at most 0.015.
Values may be sent and summed in bfloat16 or wider, within the bound.
A program may use at most 128 MiB of HBM per device.

```python
import math
import jax
import jax.numpy as jnp
from jax import lax

NX = 512
NY = 512
NZ = 256
KZ = 128
NBINS = 4
N_SPEC = 2


def with_ends(array, rng, least, largest):
    extent = array.shape
    index_at = [jax.random.randint(jax.random.fold_in(rng, axis), (), 0, extent[axis]) for axis in range(len(extent))]
    array = array.at[tuple(index_at)].set(least)
    longest = extent.index(max(extent))
    index_at[longest] = (index_at[longest] + 1) % extent[longest]
    return array.at[tuple(index_at)].set(largest)


def shard_levels(key, shape, cuts, least, high):
    gain = 1.0
    for dim, shards_of in cuts:
        heights = jax.random.uniform(jax.random.fold_in(jax.random.fold_in(key, 6), dim), (shards_of,), jnp.float32, least / len(cuts), high / len(cuts))
        gain = gain * jnp.repeat(jnp.exp(heights), shape[dim] // shards_of).reshape((-1,) + (1,) * (len(shape) - 1 - dim))
    return gain


def centred(stream_key, shape, deviation, reach, shards=(), held_as=jnp.bfloat16):
    array = jax.random.normal(stream_key, shape, jnp.float32) * deviation
    if len(shards) > 0:
        array = shard_levels(stream_key, shape, shards, -0.22, 0.18) * array
    return jnp.clip(array, min=-reach, max=reach).astype(held_as)


def setup_inputs(seed: int = 0) -> dict:
    key_of = jax.random.split(jax.random.key(seed), 8)
    return {
        "amplitude": jnp.clip(0.5 + 1.0 * jax.random.uniform(key_of[0], (NX, NY, NZ), jnp.float32) ** shard_levels(key_of[0], (NX, NY, NZ), ((0, 64),), -0.2, 0.2), 0.5, 1.5).astype(jnp.bfloat16),
        "displacement": centred(key_of[1], (3, NX, NY, NZ), 1.0, 4.0, ((1, 64),)),
        "support": with_ends((jax.random.randint(key_of[2], (NX, NY, NZ), 0, 4) < 3).astype(jnp.int32), jax.random.fold_in(key_of[2], 1), 0, 1),
        "counts": with_ends(jax.random.randint(key_of[3], (NX, NY, KZ), 0, 12), jax.random.fold_in(key_of[3], 1), 0, 11).astype(jnp.int32),
        "bin_weights": jnp.clip(jnp.exp(jax.random.uniform(key_of[4], (NBINS,), jnp.float32, math.log(0.5), math.log(2.0))), 0.5, 2.0),
        "bin_scales": jnp.clip(jax.random.uniform(key_of[5], (NBINS,), jnp.float32, 0.96, 1.04), 0.96, 1.04),
        "bragg_vector": jnp.clip(jax.random.uniform(key_of[6], (3,), jnp.float32, 1.0, 3.0), 1.0, 3.0),
    }


step_size = 0.5

def chirp_matrix(count_out, count_in, bin_scale):
    out_offset = jnp.arange(count_out, dtype=jnp.int32) - count_out // 2
    in_offset = jnp.arange(count_in, dtype=jnp.int32) - count_in // 2
    product = out_offset[:, None] * in_offset[None, :]
    fraction = (product % count_in).astype(jnp.float32) / count_in
    excess_angle = (bin_scale - 1.0) * (product.astype(jnp.float32) / count_in)
    phase_angle = -2.0 * math.pi * (fraction + excess_angle)
    normalizer = 1.0 / math.sqrt(count_in)
    real_part = jnp.cos(phase_angle) * normalizer
    imag_part = jnp.sin(phase_angle) * normalizer
    block_matrix = jnp.stack([jnp.stack([real_part, -imag_part]), jnp.stack([imag_part, real_part])])
    return jnp.transpose(block_matrix, (0, 2, 1, 3)).astype(jnp.bfloat16)

def rounded(values):
    return lax.optimization_barrier(values.astype(jnp.bfloat16)).astype(jnp.float32)

def reference(amplitude, displacement, support, counts, bin_weights, bin_scales, bragg_vector):
    bins_group = NBINS // N_SPEC
    amp_values = amplitude.astype(jnp.float32)
    disp_values = displacement.astype(jnp.float32)
    mask_values = support.astype(jnp.float32)
    phase_field = bragg_vector[0] * disp_values[0] + bragg_vector[1] * disp_values[1] + bragg_vector[2] * disp_values[2]
    magnitude = mask_values * amp_values
    far_list = []
    intensity = jnp.zeros((NX, NY, KZ), jnp.float32)
    for member in range(NBINS):
        bin_scale = bin_scales[member]
        bin_phase = bin_scale * phase_field
        exit_wave = rounded(jnp.stack([magnitude * jnp.cos(bin_phase), magnitude * jnp.sin(bin_phase)]))
        mat_z = chirp_matrix(KZ, NZ, bin_scale).astype(jnp.float32)
        mat_y = chirp_matrix(NY, NY, bin_scale).astype(jnp.float32)
        mat_x = chirp_matrix(NX, NX, bin_scale).astype(jnp.float32)
        section_one = rounded(jnp.einsum('pxyn,okpn->oxyk', exit_wave, mat_z, preferred_element_type=jnp.float32))
        section_two = rounded(jnp.einsum('pxnk,ojpn->oxjk', section_one, mat_y, preferred_element_type=jnp.float32))
        far_field = jnp.einsum('pnjk,oipn->oijk', section_two, mat_x, preferred_element_type=jnp.float32)
        far_list.append(far_field)
        intensity = intensity + bin_weights[member] * (far_field[0] * far_field[0] + far_field[1] * far_field[1])
    modulus_ratio = 1.0 - jnp.sqrt(counts.astype(jnp.float32) / jnp.maximum(intensity, 0.5))
    sum_amp = jnp.zeros((NX, NY, NZ), jnp.float32)
    sum_phase = jnp.zeros((NX, NY, NZ), jnp.float32)
    for group in range(N_SPEC):
        part_amp = jnp.zeros((NX, NY, NZ), jnp.float32)
        part_phase = jnp.zeros((NX, NY, NZ), jnp.float32)
        for member in range(group * bins_group, (group + 1) * bins_group):
            bin_scale = bin_scales[member]
            bin_phase = bin_scale * phase_field
            mat_z = chirp_matrix(KZ, NZ, bin_scale).astype(jnp.float32)
            mat_y = chirp_matrix(NY, NY, bin_scale).astype(jnp.float32)
            mat_x = chirp_matrix(NX, NX, bin_scale).astype(jnp.float32)
            back_field = rounded(bin_weights[member] * modulus_ratio * far_list[member])
            back_one = rounded(jnp.einsum('oijk,oipn->pnjk', back_field, mat_x, preferred_element_type=jnp.float32))
            back_two = rounded(jnp.einsum('oxjk,ojpn->pxnk', back_one, mat_y, preferred_element_type=jnp.float32))
            back_three = jnp.einsum('oxyk,okpn->pxyn', back_two, mat_z, preferred_element_type=jnp.float32)
            cosine = jnp.cos(bin_phase)
            sine_part = jnp.sin(bin_phase)
            part_amp = part_amp + (back_three[0] * cosine + back_three[1] * sine_part)
            part_phase = part_phase + bin_scale * (back_three[0] * sine_part - back_three[1] * cosine)
        sum_amp = sum_amp + rounded(part_amp)
        sum_phase = sum_phase + rounded(part_phase)
    new_amplitude = amp_values - step_size * (mask_values * sum_amp)
    grad_phase = -mask_values * amp_values * sum_phase
    new_displacement = (disp_values - step_size * bragg_vector[:, None, None, None] * grad_phase[None]).astype(jnp.bfloat16)
    return (new_amplitude, new_displacement)
```

```python
import functools
import math

import jax
import jax.numpy as jnp
from jax import lax
from jax.experimental import pallas as pl
from jax.experimental.pallas import tpu as pltpu
from jax.sharding import PartitionSpec as P

step_size = 0.5
both_axes = ("slab", "spec")
vmem_limit = 60 * 1024 * 1024
cos_terms = (
    0.9999992117703129, -19.738980419471183, 64.92865850463387,
    -85.27162830147759, 58.7905066287335, -21.071108461812614,
)
sin_terms = (
    6.283184916984337, -41.34158926418227, 81.59994386457431,
    -76.61447586037943, 41.342889429509576, -12.4712447471884,
)


def cos_sin_turns(turns):
    rest = turns - jnp.floor(turns + 0.5)
    square = rest * rest
    cosine = jnp.full_like(square, cos_terms[-1])
    sine = jnp.full_like(square, sin_terms[-1])
    for level in range(len(cos_terms) - 2, -1, -1):
        cosine = cosine * square + cos_terms[level]
        sine = sine * square + sin_terms[level]
    return cosine, sine * rest


def chirp_parts(out_index, in_index, count_out, count_in, bin_scale):
    product = (out_index - count_out // 2) * (in_index - count_in // 2)
    fraction = (product & (count_in - 1)).astype(jnp.float32) * (1.0 / count_in)
    excess = (bin_scale - 1.0) * (product.astype(jnp.float32) * (1.0 / count_in))
    cosine, sine = cos_sin_turns(fraction + excess)
    normalizer = 1.0 / math.sqrt(count_in)
    return cosine * normalizer, sine * -normalizer


def iota(shape, dim):
    return lax.broadcasted_iota(jnp.int32, shape, dim)


def dot(a, b):
    return jnp.dot(a, b, preferred_element_type=jnp.float32)


def params(limit=vmem_limit):
    return pltpu.CompilerParams(vmem_limit_bytes=limit)


def row_matrices_kernel(scales_ref, rows_ref, zf_ref, zb_ref, *, size, cells_z, frames):
    bin_scale = scales_ref[pl.program_id(0)]
    tile = 64

    def body(step, carry):
        start = step * tile
        out_index = start + iota((tile, size), 0)
        real, imag = chirp_parts(out_index, iota((tile, size), 1), size, size, bin_scale)
        real = real.reshape(tile // 8, 8, size)
        imag = imag.reshape(tile // 8, 8, size)
        low = iota(real.shape, 1) < 4

        def interleave(first, second):
            even = jnp.where(low, first, pltpu.roll(second, 4, 1))
            odd = jnp.where(low, pltpu.roll(first, 4, 1), second)
            return jnp.stack([even, odd], axis=1).reshape(2 * tile, size)

        at = pl.ds(pl.multiple_of(2 * start, 2 * tile), 2 * tile)
        rows_ref[0, at, 0:size] = interleave(real, imag).astype(jnp.bfloat16)
        rows_ref[0, at, size : 2 * size] = interleave(-imag, real).astype(jnp.bfloat16)
        return carry

    lax.fori_loop(0, size // tile, body, 0)
    real, imag = chirp_parts(
        iota((cells_z, frames), 1), iota((cells_z, frames), 0), frames, cells_z, bin_scale
    )
    zf_ref[0, 0:cells_z, 0:frames] = real.astype(jnp.bfloat16)
    zf_ref[0, 0:cells_z, frames : 2 * frames] = imag.astype(jnp.bfloat16)
    zf_ref[0, cells_z : 2 * cells_z, 0:frames] = (-imag).astype(jnp.bfloat16)
    zf_ref[0, cells_z : 2 * cells_z, frames : 2 * frames] = real.astype(jnp.bfloat16)
    real, imag = chirp_parts(
        iota((frames, cells_z), 0), iota((frames, cells_z), 1), frames, cells_z, bin_scale
    )
    zb_ref[0, 0:frames, 0:cells_z] = real.astype(jnp.bfloat16)
    zb_ref[0, 0:frames, cells_z : 2 * cells_z] = imag.astype(jnp.bfloat16)
    zb_ref[0, frames : 2 * frames, 0:cells_z] = (-imag).astype(jnp.bfloat16)
    zb_ref[0, frames : 2 * frames, cells_z : 2 * cells_z] = real.astype(jnp.bfloat16)


def row_matrices(bin_scales, size, cells_z, frames):
    bins = bin_scales.shape[0]
    return pl.pallas_call(
        functools.partial(row_matrices_kernel, size=size, cells_z=cells_z, frames=frames),
        grid=(bins,),
        in_specs=[pl.BlockSpec(memory_space=pltpu.SMEM)],
        out_specs=[
            pl.BlockSpec((1, 2 * size, 2 * size), lambda b: (b, 0, 0)),
            pl.BlockSpec((1, 2 * cells_z, 2 * frames), lambda b: (b, 0, 0)),
            pl.BlockSpec((1, 2 * frames, 2 * cells_z), lambda b: (b, 0, 0)),
        ],
        out_shape=[
            jax.ShapeDtypeStruct((bins, 2 * size, 2 * size), jnp.bfloat16),
            jax.ShapeDtypeStruct((bins, 2 * cells_z, 2 * frames), jnp.bfloat16),
            jax.ShapeDtypeStruct((bins, 2 * frames, 2 * cells_z), jnp.bfloat16),
        ],
        compiler_params=params(),
        name="row_matrices",
    )(bin_scales)


def column_matrices_kernel(scales_ref, cols_ref, *, size):
    bin_scale = scales_ref[pl.program_id(0)]
    tile = 64
    owners = size // 4

    def body(step, carry):
        start = step * tile
        out_index = start + iota((tile, size), 0)
        lane = iota((tile, size), 1)
        in_index = 4 * (lane % owners) + lane // owners
        real, imag = chirp_parts(out_index, in_index, size, size, bin_scale)
        at = pl.ds(pl.multiple_of(start, tile), tile)
        cols_ref[0, 0, at, 0:size] = real.astype(jnp.bfloat16)
        cols_ref[0, 0, at, size : 2 * size] = (-imag).astype(jnp.bfloat16)
        cols_ref[0, 1, at, 0:size] = imag.astype(jnp.bfloat16)
        cols_ref[0, 1, at, size : 2 * size] = real.astype(jnp.bfloat16)
        return carry

    lax.fori_loop(0, size // tile, body, 0)


def column_matrices(bin_scales, size):
    bins = bin_scales.shape[0]
    return pl.pallas_call(
        functools.partial(column_matrices_kernel, size=size),
        grid=(bins,),
        in_specs=[pl.BlockSpec(memory_space=pltpu.SMEM)],
        out_specs=pl.BlockSpec((1, 2, size, 2 * size), lambda b: (b, 0, 0, 0)),
        out_shape=jax.ShapeDtypeStruct((bins, 2, size, 2 * size), jnp.bfloat16),
        compiler_params=params(),
        cost_estimate=pl.CostEstimate(flops=8_000_000_000, bytes_accessed=8 << 20, transcendentals=0),
        name="column_matrices",
    )(bin_scales)


def forward_kernel(
    place_ref, bragg_ref, scales_ref, disp_ref, amp_ref, mask_ref, zf_ref, rows_ref,
    wave_ref, out_ref, section, *, first,
):
    step = pl.program_id(0)
    cells_y, cells_z = amp_ref.shape[1:]
    frames = zf_ref.shape[2] // 2

    @pl.when(step < 4)
    def _():
        phase = (
            bragg_ref[0] * disp_ref[0, 0].astype(jnp.float32)
            + bragg_ref[1] * disp_ref[1, 0].astype(jnp.float32)
            + bragg_ref[2] * disp_ref[2, 0].astype(jnp.float32)
        )
        magnitude = amp_ref[0].astype(jnp.float32) * mask_ref[0].astype(jnp.float32)
        for member in range(2):
            scale = scales_ref[first + member] * (0.5 / math.pi)
            cosine, sine = cos_sin_turns(scale * phase)
            wave_ref[member, 0, :, 0:cells_z] = (magnitude * cosine).astype(jnp.bfloat16)
            wave_ref[member, 0, :, cells_z : 2 * cells_z] = (magnitude * sine).astype(jnp.bfloat16)
            both = dot(wave_ref[member, 0], zf_ref[member]).astype(jnp.bfloat16)
            section[member, step, 0:cells_y, :] = both[:, 0:frames]
            section[member, step, cells_y : 2 * cells_y, :] = both[:, frames : 2 * frames]

    @pl.when(step >= 4)
    def _():
        parts = []
        for member in range(2):
            wide = jnp.concatenate([section[member, row] for row in range(4)], axis=1)
            value = dot(rows_ref[member], wide)
            parts.append(value.reshape(value.shape[0] // 8, 8, value.shape[1]))
        out_ref[...] = jnp.concatenate(parts, axis=1).astype(jnp.bfloat16)


def forward(place, bragg, scales, disp, amp, mask, zf, rows, first):
    _, _, cells_y, cells_z = disp.shape
    size = rows.shape[1]
    frames = zf.shape[2] // 2
    pair = first // 2
    tiles = 4
    row_tile = size // tiles
    owners = size // 8

    def at_row(step):
        return jnp.minimum(step, 3)

    def at_tile(step):
        return jnp.maximum(step - 4, 0)

    return pl.pallas_call(
        functools.partial(forward_kernel, first=first),
        grid_spec=pltpu.PrefetchScalarGridSpec(
            num_scalar_prefetch=3,
            grid=(4 + tiles,),
            in_specs=[
                pl.BlockSpec((3, 1, cells_y, cells_z), lambda t, p, *_: (0, 4 * p[0] + at_row(t), 0, 0)),
                pl.BlockSpec((1, cells_y, cells_z), lambda t, p, *_: (4 * p[0] + at_row(t), 0, 0)),
                pl.BlockSpec((1, cells_y, cells_z), lambda t, p, *_: (4 * p[0] + at_row(t), 0, 0)),
                pl.BlockSpec((2, 2 * cells_z, 2 * frames), lambda t, *_: (pair, 0, 0)),
                pl.BlockSpec((2, row_tile, size), lambda t, *_: (pair, at_tile(t), 0)),
            ],
            out_specs=[
                pl.BlockSpec((2, 1, cells_y, 2 * cells_z), lambda t, *_: (0, at_row(t), 0, 0)),
                pl.BlockSpec((owners // tiles, 16, 4 * frames), lambda t, *_: (at_tile(t), 0, 0)),
            ],
            scratch_shapes=[pltpu.VMEM((2, 4, 2 * cells_y, frames), jnp.bfloat16)],
        ),
        out_shape=[
            jax.ShapeDtypeStruct((2, 4, cells_y, 2 * cells_z), jnp.bfloat16),
            jax.ShapeDtypeStruct((owners, 16, 4 * frames), jnp.bfloat16),
        ],
        compiler_params=params(),
        cost_estimate=pl.CostEstimate(flops=3_300_000_000 * 2, bytes_accessed=20 << 20, transcendentals=0),
        name="forward_z_y",
    )(place, bragg, scales, disp, amp, mask, zf, rows)


def gather_columns(got_ref, wide, frames):
    owners = got_ref.shape[0]
    for lane_group in range(4):
        piece = got_ref[:, :, lane_group * frames : (lane_group + 1) * frames]
        turned = jnp.swapaxes(piece.astype(jnp.float32), 0, 1).astype(jnp.bfloat16)
        for member in range(2):
            for part in range(2):
                at = (4 * part + lane_group) * owners
                for row in range(4):
                    wide[member, at : at + owners, row * frames : (row + 1) * frames] = turned[
                        8 * member + 4 * part + row
                    ]


def far_kernel(got_ref, cols_ref, out_ref, wide, *, frames):
    step = pl.program_id(0)

    @pl.when(step == 0)
    def _():
        gather_columns(got_ref, wide, frames)

    for member in range(2):
        for part in range(2):
            out_ref[member, part] = dot(cols_ref[member, part], wide[member]).astype(out_ref.dtype)


def apply_columns(got, cols, first, out_dtype):
    owners, _, lanes = got.shape
    size = cols.shape[2]
    frames = lanes // 4
    tiles = 4
    pair = first // 2
    return pl.pallas_call(
        functools.partial(far_kernel, frames=frames),
        grid=(tiles,),
        in_specs=[
            pl.BlockSpec((owners, 16, lanes), lambda t: (0, 0, 0)),
            pl.BlockSpec((2, 2, size // tiles, 2 * size), lambda t: (pair, 0, t, 0)),
        ],
        out_specs=pl.BlockSpec((2, 2, size // tiles, lanes), lambda t: (0, 0, t, 0)),
        out_shape=jax.ShapeDtypeStruct((2, 2, size, lanes), out_dtype),
        scratch_shapes=[pltpu.VMEM((2, 2 * size, lanes), jnp.bfloat16)],
        compiler_params=params(),
        cost_estimate=pl.CostEstimate(flops=4_300_000_000, bytes_accessed=12 << 20, transcendentals=0),
        name="apply_columns",
    )(got, cols)


def ratio_kernel(weights_ref, low_ref, high_ref, counts_ref, back_low_ref, back_high_ref):
    intensity = None
    for member in range(4):
        field_ref = low_ref if member < 2 else high_ref
        real, imag = field_ref[member % 2, 0], field_ref[member % 2, 1]
        term = weights_ref[member] * (real * real + imag * imag)
        intensity = term if intensity is None else intensity + term
    ratio = 1.0 - jnp.sqrt(counts_ref[...].astype(jnp.float32) / jnp.maximum(intensity, 0.5))
    for member in range(4):
        field_ref = low_ref if member < 2 else high_ref
        back_ref = back_low_ref if member < 2 else back_high_ref
        factor = weights_ref[member] * ratio
        back_ref[member % 2, 0] = (factor * field_ref[member % 2, 0]).astype(jnp.bfloat16)
        back_ref[member % 2, 1] = (-factor * field_ref[member % 2, 1]).astype(jnp.bfloat16)


def back_fields(weights, low, high, counts):
    _, _, size, lanes = low.shape
    tiles = 8
    field = pl.BlockSpec((2, 2, size // tiles, lanes), lambda t: (0, 0, t, 0))
    return pl.pallas_call(
        ratio_kernel,
        grid=(tiles,),
        in_specs=[
            pl.BlockSpec(memory_space=pltpu.SMEM),
            field,
            field,
            pl.BlockSpec((size // tiles, lanes), lambda t: (t, 0)),
        ],
        out_specs=[field, field],
        out_shape=[jax.ShapeDtypeStruct(low.shape, jnp.bfloat16)] * 2,
        compiler_params=params(),
        name="back_fields",
    )(weights, low, high, counts)


def back_rows_kernel(field_ref, rows_ref, out_ref):
    parts = []
    for member in range(2):
        value = dot(rows_ref[member], field_ref[member])
        parts.append(value.reshape(value.shape[0] // 8, 8, value.shape[1]))
    out_ref[...] = jnp.concatenate(parts, axis=1).astype(jnp.bfloat16)


def back_rows(field, rows, first):
    size = rows.shape[1]
    lanes = field.shape[3]
    tiles = 4
    pair = first // 2
    owners = size // 8
    return pl.pallas_call(
        back_rows_kernel,
        grid=(tiles,),
        in_specs=[
            pl.BlockSpec((2, size, lanes), lambda t: (0, 0, 0)),
            pl.BlockSpec((2, size // tiles, size), lambda t: (pair, t, 0)),
        ],
        out_specs=pl.BlockSpec((owners // tiles, 16, lanes), lambda t: (t, 0, 0)),
        out_shape=jax.ShapeDtypeStruct((owners, 16, lanes), jnp.bfloat16),
        compiler_params=params(),
        cost_estimate=pl.CostEstimate(flops=4_300_000_000, bytes_accessed=8 << 20, transcendentals=0),
        name="back_rows",
    )(field.reshape(2, size, lanes), rows)


def gradient_kernel(place_ref, scales_ref, low_ref, high_ref, zb_ref, wave_low_ref, wave_high_ref, amp_ref, out_ref):
    cells_y, cells_z = amp_ref.shape[1:]
    sum_amp = None
    sum_phase = None
    for member in range(4):
        field_ref = low_ref if member < 2 else high_ref
        wave_ref = wave_low_ref if member < 2 else wave_high_ref
        field = jnp.concatenate([field_ref[member % 2, 0], field_ref[member % 2, 1]], axis=1)
        both = dot(field, zb_ref[member])
        back_real, back_imag = both[:, 0:cells_z], both[:, cells_z : 2 * cells_z]
        wave_real = wave_ref[member % 2, 0, :, 0:cells_z].astype(jnp.float32)
        wave_imag = wave_ref[member % 2, 0, :, cells_z : 2 * cells_z].astype(jnp.float32)
        term_amp = back_real * wave_real - back_imag * wave_imag
        term_phase = scales_ref[member] * (back_real * wave_imag + back_imag * wave_real)
        sum_amp = term_amp if sum_amp is None else sum_amp + term_amp
        sum_phase = term_phase if sum_phase is None else sum_phase + term_phase
    out_ref[0, 0] = (sum_amp / amp_ref[0].astype(jnp.float32)).astype(jnp.bfloat16)
    out_ref[0, 1] = sum_phase.astype(jnp.bfloat16)


def gradient(place, scales, low, high, zb, wave_low, wave_high, amp, first_row, rows):
    _, cells_y, cells_z = amp.shape
    frames = zb.shape[1] // 2
    size = low.shape[2]
    field = pl.BlockSpec((2, 2, size, frames), lambda t, *_: (0, 0, 0, first_row + t))
    wave = pl.BlockSpec((2, 1, cells_y, 2 * cells_z), lambda t, *_: (0, first_row + t, 0, 0))
    return pl.pallas_call(
        gradient_kernel,
        grid_spec=pltpu.PrefetchScalarGridSpec(
            num_scalar_prefetch=2,
            grid=(rows,),
            in_specs=[
                field,
                field,
                pl.BlockSpec(zb.shape, lambda t, *_: (0, 0, 0)),
                wave,
                wave,
                pl.BlockSpec((1, cells_y, cells_z), lambda t, p, *_: (4 * p[0] + first_row + t, 0, 0)),
            ],
            out_specs=pl.BlockSpec((1, 2, cells_y, cells_z), lambda t, *_: (t, 0, 0, 0)),
        ),
        out_shape=jax.ShapeDtypeStruct((rows, 2, cells_y, cells_z), jnp.bfloat16),
        compiler_params=params(),
        cost_estimate=pl.CostEstimate(flops=1_000_000_000 * rows, bytes_accessed=(6 << 20) * rows, transcendentals=0),
        name="gradient",
    )(place, scales, low, high, zb, wave_low, wave_high, amp)


def finish_kernel(place_ref, bragg_ref, sums_ref, amp_ref, disp_ref, *rest):
    new_amp_ref, new_disp_ref = rest[-2:]
    new_amp_ref[0] = amp_ref[0].astype(jnp.float32) - step_size * sums_ref[0, 0].astype(jnp.float32)
    sum_phase = sums_ref[0, 1].astype(jnp.float32)
    for axis in range(3):
        new_disp_ref[axis, 0] = (
            disp_ref[axis, 0].astype(jnp.float32) + (step_size * bragg_ref[axis]) * sum_phase
        ).astype(jnp.bfloat16)


def finish(place, bragg, sums, amp, disp, earlier, first_row, other):
    rows = sums.shape[0]
    _, cells_y, cells_z = amp.shape

    def row(t, p):
        half = 1 - p[0] if other else p[0]
        return 4 * half + first_row + t

    amp_spec = pl.BlockSpec((1, cells_y, cells_z), lambda t, p, *_: (row(t, p), 0, 0))
    disp_spec = pl.BlockSpec((3, 1, cells_y, cells_z), lambda t, p, *_: (0, row(t, p), 0, 0))
    kept = [] if earlier is None else list(earlier)
    return pl.pallas_call(
        finish_kernel,
        grid_spec=pltpu.PrefetchScalarGridSpec(
            num_scalar_prefetch=2,
            grid=(rows,),
            in_specs=[
                pl.BlockSpec((1, 2, cells_y, cells_z), lambda t, *_: (t, 0, 0, 0)),
                amp_spec,
                disp_spec,
            ]
            + [pl.BlockSpec(memory_space=pl.ANY)] * len(kept),
            out_specs=[amp_spec, disp_spec],
        ),
        out_shape=[
            jax.ShapeDtypeStruct(amp.shape, jnp.float32),
            jax.ShapeDtypeStruct(disp.shape, jnp.bfloat16),
        ],
        input_output_aliases={} if earlier is None else {5: 0, 6: 1},
        compiler_params=params(),
        cost_estimate=pl.CostEstimate(flops=10_000_000, bytes_accessed=(3 << 20) * rows, transcendentals=0),
        name="finish",
    )(place, bragg, sums, amp, disp, *kept)


def exchange(blocks):
    return lax.all_to_all(blocks, both_axes, split_axis=0, concat_axis=0, tiled=True)


def swap(values):
    return lax.ppermute(values, "spec", [(0, 1), (1, 0)])


def per_device(amplitude, displacement, support, counts, bin_weights, bin_scales, bragg_vector):
    place = lax.axis_index("spec").reshape(1).astype(jnp.int32)
    size, rows_y, frames = counts.shape
    cells_z = amplitude.shape[2]
    rows, zf, zb = row_matrices(bin_scales, size, cells_z, frames)
    waves, sent = [], []
    for first in (0, 2):
        wave, blocks = forward(
            place, bragg_vector, bin_scales, displacement, amplitude, support, zf, rows, first
        )
        waves.append(wave)
        sent.append(exchange(blocks))
    cols = column_matrices(bin_scales, size)
    my_counts = lax.dynamic_slice_in_dim(counts, place[0] * (rows_y // 2), rows_y // 2, axis=1)
    my_counts = my_counts.reshape(size, rows_y // 2 * frames)
    far = [apply_columns(sent[k], cols, 2 * k, jnp.float32) for k in range(2)]
    fields = back_fields(bin_weights, far[0], far[1], my_counts)
    returned = [exchange(back_rows(fields[k], rows, 2 * k)) for k in range(2)]
    back = [apply_columns(returned[k], cols, 2 * k, jnp.bfloat16) for k in range(2)]
    outs = None
    sums = []
    for first_row in (0, 2):
        part = gradient(
            place, bin_scales, back[0], back[1], zb, waves[0], waves[1], amplitude, first_row, 2
        )
        sums.append((part, swap(part)))
    for other in (False, True):
        for k in range(2):
            outs = finish(
                place, bragg_vector, sums[k][other], amplitude, displacement, outs, 2 * k, other
            )
    return tuple(outs)


def solution(mesh):
    in_specs = (
        P("slab", None, None),
        P(None, "slab", None, None),
        P("slab", None, None),
        P(None, "slab", None),
        P(),
        P(),
        P(),
    )
    out_specs = (P("slab", None, None), P(None, "slab", None, None))
    return jax.shard_map(
        per_device, mesh=mesh, in_specs=in_specs, out_specs=out_specs, check_vma=False
    )
```

```python
import functools
import math

import jax
import jax.numpy as jnp
from jax import lax
from jax.experimental import pallas as pl
from jax.experimental.pallas import tpu as pltpu
from jax.sharding import PartitionSpec as P

step_size = 0.5
both_axes = ("slab", "spec")
vmem_limit = 60 * 1024 * 1024
small_limit = 36 * 1024 * 1024
cos_terms = (
    0.9999992117703129, -19.738980419471183, 64.92865850463387,
    -85.27162830147759, 58.7905066287335, -21.071108461812614,
)
sin_terms = (
    6.283184916984337, -41.34158926418227, 81.59994386457431,
    -76.61447586037943, 41.342889429509576, -12.4712447471884,
)


wave_cos_terms = (
    0.9999590619701949, -19.73094403547976, 64.67145824268955,
    -82.39085380484792, 45.6210638400798,
)
wave_sin_terms = (
    6.283161153735962, -41.33683281238831, 81.44771611530231,
    -74.90944720114622, 33.548361462485595,
)


def cos_sin_turns(turns, cos_series=cos_terms, sin_series=sin_terms):
    rest = turns - jnp.floor(turns + 0.5)
    square = rest * rest
    cosine = jnp.full_like(square, cos_series[-1])
    sine = jnp.full_like(square, sin_series[-1])
    for level in range(len(cos_series) - 2, -1, -1):
        cosine = cosine * square + cos_series[level]
        sine = sine * square + sin_series[level]
    return cosine, sine * rest


def chirp_parts(out_index, in_index, count_out, count_in, bin_scale):
    product = (out_index - count_out // 2) * (in_index - count_in // 2)
    fraction = (product & (count_in - 1)).astype(jnp.float32) * (1.0 / count_in)
    excess = (bin_scale - 1.0) * (product.astype(jnp.float32) * (1.0 / count_in))
    cosine, sine = cos_sin_turns(fraction + excess)
    normalizer = 1.0 / math.sqrt(count_in)
    return cosine * normalizer, sine * -normalizer


def iota(shape, dim):
    return lax.broadcasted_iota(jnp.int32, shape, dim)


def dot(a, b):
    return jnp.dot(a, b, preferred_element_type=jnp.float32)


def params(limit=vmem_limit):
    return pltpu.CompilerParams(vmem_limit_bytes=limit)


def small_table(index, stride, others, size, bin_scale):
    product = stride * index * others
    fraction = (product & (size - 1)).astype(jnp.float32) * (1.0 / size)
    excess = (bin_scale - 1.0) * (product.astype(jnp.float32) * (1.0 / size))
    cosine, sine = cos_sin_turns(fraction + excess)
    return cosine, -sine


def fill_tables(big_real, big_imag, lane_index, size, bin_scale):
    others = lane_index - size // 2
    wide = (size // 8, size)
    real, imag = small_table(iota(wide, 0) - size // 16, 8, jnp.broadcast_to(others, wide), size, bin_scale)
    normalizer = 1.0 / math.sqrt(size)
    big_real[...] = real * normalizer
    big_imag[...] = imag * normalizer
    narrow = (8, size)
    return small_table(iota(narrow, 0), 1, jnp.broadcast_to(others, narrow), size, bin_scale)


def table_rows(big_real, big_imag, small, step):
    real = jnp.broadcast_to(big_real[pl.ds(step, 1), :], small[0].shape)
    imag = jnp.broadcast_to(big_imag[pl.ds(step, 1), :], small[0].shape)
    return real * small[0] - imag * small[1], real * small[1] + imag * small[0]


def fill_z(zf_ref, member, bin_scale, cells_z, frames):
    real, imag = chirp_parts(
        iota((cells_z, frames), 1), iota((cells_z, frames), 0), frames, cells_z, bin_scale
    )
    zf_ref[member, 0:cells_z, 0:frames] = real.astype(jnp.bfloat16)
    zf_ref[member, 0:cells_z, frames : 2 * frames] = imag.astype(jnp.bfloat16)
    zf_ref[member, cells_z : 2 * cells_z, 0:frames] = (-imag).astype(jnp.bfloat16)
    zf_ref[member, cells_z : 2 * cells_z, frames : 2 * frames] = real.astype(jnp.bfloat16)


def row_matrices_kernel(scales_ref, rows_ref, big_real, big_imag, *, size):
    bin_scale = scales_ref[pl.program_id(0)]
    small = fill_tables(big_real, big_imag, iota((1, size), 1), size, bin_scale)
    low = (iota((8, size), 0) & 2) == 0

    def body(step, carry):
        halves = [[[], []], [[], []]]
        for sub in range(2):
            real, imag = table_rows(big_real, big_imag, small, 2 * step + sub)
            for column, (first, second) in enumerate(((real, imag), (-imag, real))):
                halves[0][column].append(jnp.where(low, first, pltpu.roll(second, 2, 0)))
                halves[1][column].append(jnp.where(low, pltpu.roll(first, 6, 0), second))
        at = pl.ds(pl.multiple_of(16 * step, 16), 16)
        for half in range(2):
            for column in range(2):
                rows_ref[0, half, at, column * size : (column + 1) * size] = jnp.concatenate(
                    halves[half][column], axis=0
                ).astype(jnp.bfloat16)
        return carry

    lax.fori_loop(0, size // 16, body, 0)


def row_matrices(bin_scales, size):
    bins = bin_scales.shape[0]
    return pl.pallas_call(
        functools.partial(row_matrices_kernel, size=size),
        grid=(bins,),
        in_specs=[pl.BlockSpec(memory_space=pltpu.SMEM)],
        out_specs=pl.BlockSpec((1, 2, size, 2 * size), lambda b: (b, 0, 0, 0)),
        out_shape=jax.ShapeDtypeStruct((bins, 2, size, 2 * size), jnp.bfloat16),
        scratch_shapes=[pltpu.VMEM((size // 8, size), jnp.float32)] * 2,
        compiler_params=params(),
        cost_estimate=pl.CostEstimate(flops=4_000_000_000, bytes_accessed=8 << 20, transcendentals=0),
        name="row_matrices",
    )(bin_scales)


def column_matrices_kernel(scales_ref, cols_ref, zb_ref, big_real, big_imag, *, size, cells_z, frames):
    bin_scale = scales_ref[pl.program_id(0)]
    owners = size // 4
    lane = iota((1, size), 1)
    small = fill_tables(big_real, big_imag, 4 * (lane % owners) + lane // owners, size, bin_scale)
    wide = size // 2

    def body(step, carry):
        pairs = [table_rows(big_real, big_imag, small, 2 * step + sub) for sub in range(2)]
        real = jnp.concatenate([pair[0] for pair in pairs], axis=0)
        imag = jnp.concatenate([pair[1] for pair in pairs], axis=0)
        at = pl.ds(pl.multiple_of(16 * step, 16), 16)
        for part, (first, second) in enumerate(((real, -imag), (imag, real))):
            for half in range(2):
                lanes = slice(half * wide, (half + 1) * wide)
                cols_ref[0, part, at, 2 * half * wide : (2 * half + 1) * wide] = first[:, lanes].astype(jnp.bfloat16)
                cols_ref[0, part, at, (2 * half + 1) * wide : (2 * half + 2) * wide] = second[:, lanes].astype(jnp.bfloat16)
        return carry

    lax.fori_loop(0, size // 16, body, 0)
    real, imag = chirp_parts(
        iota((frames, cells_z), 0), iota((frames, cells_z), 1), frames, cells_z, bin_scale
    )
    zb_ref[0, 0:frames, 0:cells_z] = real.astype(jnp.bfloat16)
    zb_ref[0, 0:frames, cells_z : 2 * cells_z] = imag.astype(jnp.bfloat16)
    zb_ref[0, frames : 2 * frames, 0:cells_z] = (-imag).astype(jnp.bfloat16)
    zb_ref[0, frames : 2 * frames, cells_z : 2 * cells_z] = real.astype(jnp.bfloat16)


def column_matrices(bin_scales, size, cells_z, frames):
    bins = bin_scales.shape[0]
    return pl.pallas_call(
        functools.partial(column_matrices_kernel, size=size, cells_z=cells_z, frames=frames),
        grid=(bins,),
        in_specs=[pl.BlockSpec(memory_space=pltpu.SMEM)],
        out_specs=[
            pl.BlockSpec((1, 2, size, 2 * size), lambda b: (b, 0, 0, 0)),
            pl.BlockSpec((1, 2 * frames, 2 * cells_z), lambda b: (b, 0, 0)),
        ],
        out_shape=[
            jax.ShapeDtypeStruct((bins, 2, size, 2 * size), jnp.bfloat16),
            jax.ShapeDtypeStruct((bins, 2 * frames, 2 * cells_z), jnp.bfloat16),
        ],
        scratch_shapes=[pltpu.VMEM((size // 8, size), jnp.float32)] * 2,
        compiler_params=params(),
        cost_estimate=pl.CostEstimate(flops=4_000_000_000, bytes_accessed=8 << 20, transcendentals=0),
        name="column_matrices",
    )(bin_scales)


def pack_owners(values, out_ref, place):
    lanes = out_ref.shape[2]
    tile = 8

    def body(step, carry):
        at = pl.ds(pl.multiple_of(step * 4 * tile, 4 * tile), 4 * tile)
        rows = [values(member, at).reshape(tile // 2, 8, lanes) for member in range(4)]
        low = iota(rows[0].shape, 1) < 4
        even, odd = [], []
        for first, second in ((rows[0], rows[1]), (rows[2], rows[3])):
            even.append(jnp.where(low, first, pltpu.roll(second, 4, 1)))
            odd.append(jnp.where(low, pltpu.roll(first, 4, 1), second))
        even = jnp.concatenate(even, axis=1)
        odd = jnp.concatenate(odd, axis=1)
        both = jnp.stack([even, odd], axis=1).reshape(tile, 16, lanes)
        out_ref[pl.ds(step * tile, tile), pl.ds(place, 16), :] = both.astype(jnp.bfloat16)
        return carry

    lax.fori_loop(0, out_ref.shape[0] // tile, body, 0)


def wave_chunk(bragg_ref, scales_ref, disp_ref, amp_ref, mask_ref, row, at, use):
    phase = (
        bragg_ref[0] * disp_ref[0, row, at, :].astype(jnp.float32)
        + bragg_ref[1] * disp_ref[1, row, at, :].astype(jnp.float32)
        + bragg_ref[2] * disp_ref[2, row, at, :].astype(jnp.float32)
    )
    magnitude = amp_ref[row, at, :].astype(jnp.float32) * mask_ref[row, at, :].astype(jnp.float32)
    for member in range(4):
        cosine, sine = cos_sin_turns(
            (scales_ref[member] * (0.5 / math.pi)) * phase, wave_cos_terms, wave_sin_terms
        )
        use(
            member,
            jnp.concatenate(
                [(magnitude * cosine).astype(jnp.bfloat16), (magnitude * sine).astype(jnp.bfloat16)], axis=1
            ),
        )


def wave_kernel(place_ref, bragg_ref, scales_ref, disp_ref, amp_ref, mask_ref, wave_ref):
    tile = 64

    def body(step, carry):
        at = pl.ds(pl.multiple_of(step * tile, tile), tile)

        def use(member, wave):
            wave_ref[member, 0, at, :] = wave

        wave_chunk(bragg_ref, scales_ref, disp_ref, amp_ref, mask_ref, 0, at, use)
        return carry

    lax.fori_loop(0, amp_ref.shape[1] // tile, body, 0)


def volume_specs(cells_y, cells_z, at_row):
    return [
        pl.BlockSpec((3, 1, cells_y, cells_z), lambda t, p, *_: (0, 4 * p[0] + at_row(t), 0, 0)),
        pl.BlockSpec((1, cells_y, cells_z), lambda t, p, *_: (4 * p[0] + at_row(t), 0, 0)),
        pl.BlockSpec((1, cells_y, cells_z), lambda t, p, *_: (4 * p[0] + at_row(t), 0, 0)),
    ]


def waves(place, bragg, scales, disp, amp, mask):
    _, _, cells_y, cells_z = disp.shape
    return pl.pallas_call(
        wave_kernel,
        grid_spec=pltpu.PrefetchScalarGridSpec(
            num_scalar_prefetch=3,
            grid=(4,),
            in_specs=volume_specs(cells_y, cells_z, lambda t: t),
            out_specs=pl.BlockSpec((4, 1, cells_y, 2 * cells_z), lambda t, *_: (0, t, 0, 0)),
        ),
        out_shape=jax.ShapeDtypeStruct((4, 4, cells_y, 2 * cells_z), jnp.bfloat16),
        compiler_params=params(),
        cost_estimate=pl.CostEstimate(flops=10_000_000_000, bytes_accessed=24 << 20, transcendentals=0),
        name="waves",
    )(place, bragg, scales, disp, amp, mask)


def first_kernel(
    place_ref, bragg_ref, scales_ref, disp_ref, amp_ref, mask_ref,
    section_ref, out_ref, section, held, zf, matrix, big_real, big_imag,
):
    step = pl.program_id(0)
    cells_y, cells_z = amp_ref.shape[1:]
    frames = zf.shape[2] // 2
    size = matrix.shape[0]

    @pl.when(step == 0)
    def _():
        for member in range(4):
            fill_z(zf, member, scales_ref[member], cells_z, frames)

    @pl.when(step < 4)
    def _():
        lanes = pl.ds(pl.multiple_of(step * frames, frames), frames)
        tile = 256

        def body(turn, carry):
            at = pl.ds(pl.multiple_of(turn * tile, tile), tile)
            low = pl.ds(pl.multiple_of(cells_y + turn * tile, tile), tile)

            def use(member, wave):
                both = dot(wave, zf[member]).astype(jnp.bfloat16)
                section[member, at, lanes] = both[:, 0:frames]
                section[member, low, lanes] = both[:, frames : 2 * frames]

            wave_chunk(bragg_ref, scales_ref, disp_ref, amp_ref, mask_ref, 0, at, use)
            return carry

        lax.fori_loop(0, cells_y // tile, body, 0)

    @pl.when(step >= 4)
    def _():
        small = fill_tables(big_real, big_imag, iota((1, size), 1), size, scales_ref[step - 4])
        low = (iota((8, size), 0) & 2) == 0

        def body(turn, carry):
            columns = [[], []]
            for sub in range(2):
                real, imag = table_rows(big_real, big_imag, small, 2 * turn + sub)
                columns[0].append(jnp.where(low, real, pltpu.roll(imag, 2, 0)))
                columns[1].append(jnp.where(low, -imag, pltpu.roll(real, 2, 0)))
            at = pl.ds(pl.multiple_of(16 * turn, 16), 16)
            for column in range(2):
                matrix[at, column * size : (column + 1) * size] = jnp.concatenate(
                    columns[column], axis=0
                ).astype(jnp.bfloat16)
            return carry

        lax.fori_loop(0, size // 16, body, 0)
        section_ref[0] = section[step - 4]
        held[step - 4] = dot(matrix[...], section[step - 4])

    @pl.when(step == 7)
    def _():
        pack_owners(lambda member, at: held[member, at, :], out_ref, 0)


def first_half(place, bragg, scales, disp, amp, mask, size, frames):
    _, _, cells_y, cells_z = disp.shape
    owners = size // 4
    return pl.pallas_call(
        first_kernel,
        grid_spec=pltpu.PrefetchScalarGridSpec(
            num_scalar_prefetch=3,
            grid=(8,),
            in_specs=volume_specs(cells_y, cells_z, lambda t: jnp.minimum(t, 3)),
            out_specs=[
                pl.BlockSpec((1, 2 * cells_y, 4 * frames), lambda t, *_: (jnp.maximum(t - 4, 0), 0, 0)),
                pl.BlockSpec((owners, 16, 4 * frames), lambda t, *_: (0, 0, 0)),
            ],
            scratch_shapes=[
                pltpu.VMEM((4, 2 * cells_y, 4 * frames), jnp.bfloat16),
                pltpu.VMEM((4, size, 4 * frames), jnp.float32),
                pltpu.VMEM((4, 2 * cells_z, 2 * frames), jnp.bfloat16),
                pltpu.VMEM((size, 2 * size), jnp.bfloat16),
                pltpu.VMEM((size // 8, size), jnp.float32),
                pltpu.VMEM((size // 8, size), jnp.float32),
            ],
        ),
        out_shape=[
            jax.ShapeDtypeStruct((4, 2 * cells_y, 4 * frames), jnp.bfloat16),
            jax.ShapeDtypeStruct((owners, 16, 4 * frames), jnp.bfloat16),
        ],
        compiler_params=params(),
        cost_estimate=pl.CostEstimate(flops=9_000_000_000, bytes_accessed=14 << 20, transcendentals=0),
        name="first_half",
    )(place, bragg, scales, disp, amp, mask)


def second_kernel(section_ref, rows_ref, out_ref, held):
    step = pl.program_id(0)
    held[step] = dot(rows_ref[0, 0], section_ref[0])

    @pl.when(step == 3)
    def _():
        pack_owners(lambda member, at: held[member, at, :], out_ref, 0)


def second_half(section, rows):
    size = rows.shape[2]
    lanes = section.shape[2]
    owners = size // 4
    return pl.pallas_call(
        second_kernel,
        grid=(4,),
        in_specs=[
            pl.BlockSpec((1, 2 * size, lanes), lambda t: (t, 0, 0)),
            pl.BlockSpec((1, 1, size, 2 * size), lambda t: (t, 1, 0, 0)),
        ],
        out_specs=pl.BlockSpec((owners, 16, lanes), lambda t: (0, 0, 0)),
        out_shape=jax.ShapeDtypeStruct((owners, 16, lanes), jnp.bfloat16),
        scratch_shapes=[pltpu.VMEM((4, size, lanes), jnp.float32)],
        compiler_params=params(),
        cost_estimate=pl.CostEstimate(flops=3_000_000_000, bytes_accessed=10 << 20, transcendentals=0),
        name="second_half",
    )(section, rows)


def middle_kernel(weights_ref, got_ref, counts_ref, cols_ref, rows_ref, *rest):
    out_refs, (wide, far, back, held) = rest[:-4], rest[-4:]
    step = pl.program_id(0)
    owners = got_ref.shape[0]
    size = far.shape[2]
    frames = got_ref.shape[2] // 4
    lanes = 2 * frames

    @pl.when(step == 0)
    def _():
        for group in range(4):
            piece = got_ref[:, :, group * frames : (group + 1) * frames].astype(jnp.float32)
            turned = jnp.swapaxes(piece, 0, 1).astype(jnp.bfloat16)
            for member in range(4):
                for part in range(2):
                    at = (4 * (group // 2) + 2 * part + group % 2) * owners
                    for row in range(2):
                        wide[member, at : at + owners, row * frames : (row + 1) * frames] = turned[
                            4 * member + 2 * part + row
                        ]

    @pl.when(step < 4)
    def _():
        for part in range(2):
            far[step, part] = dot(cols_ref[0, part], wide[step])

    @pl.when(step == 3)
    def _():
        def body(turn, carry):
            at = pl.ds(pl.multiple_of(turn * 16, 16), 16)
            fields = [(far[member, 0, at, :], far[member, 1, at, :]) for member in range(4)]
            intensity = None
            for member, (real, imag) in enumerate(fields):
                term = weights_ref[member] * (real * real + imag * imag)
                intensity = term if intensity is None else intensity + term
            ratio = 1.0 - jnp.sqrt(counts_ref[at, :].astype(jnp.float32) / jnp.maximum(intensity, 0.5))
            for member, (real, imag) in enumerate(fields):
                factor = weights_ref[member] * ratio
                back[member, at, :] = (factor * real).astype(jnp.bfloat16)
                low = pl.ds(pl.multiple_of(size + turn * 16, 16), 16)
                back[member, low, :] = (-factor * imag).astype(jnp.bfloat16)
            return carry

        lax.fori_loop(0, size // 16, body, 0)

    @pl.when(step >= 4)
    def _():
        for half in range(2):
            held[step - 4, half] = dot(rows_ref[0, half], back[step - 4])

    @pl.when(step == 7)
    def _():
        for half in range(2):
            out_ref, place = (out_refs[0], 16 * half) if len(out_refs) == 1 else (out_refs[half], 0)
            pack_owners(lambda member, at, half=half: held[member, half, at, :], out_ref, place)


def middle(weights, got, counts, cols, rows, split):
    owners, _, lanes4 = got.shape
    size = rows.shape[2]
    lanes = lanes4 // 2
    if split:
        shapes = [(owners, 16, lanes)] * 2
    else:
        shapes = [(owners, 32, lanes)]
    return pl.pallas_call(
        middle_kernel,
        grid=(8,),
        in_specs=[
            pl.BlockSpec(memory_space=pltpu.SMEM),
            pl.BlockSpec(got.shape, lambda t: (0, 0, 0)),
            pl.BlockSpec(counts.shape, lambda t: (0, 0)),
            pl.BlockSpec((1, 2, size, 2 * size), lambda t: (jnp.minimum(t, 3), 0, 0, 0)),
            pl.BlockSpec((1, 2, size, 2 * size), lambda t: (jnp.maximum(t - 4, 0), 0, 0, 0)),
        ],
        out_specs=[pl.BlockSpec(shape, lambda t: (0, 0, 0)) for shape in shapes],
        out_shape=[jax.ShapeDtypeStruct(shape, jnp.bfloat16) for shape in shapes],
        scratch_shapes=[
            pltpu.VMEM((4, 2 * size, lanes), jnp.bfloat16),
            pltpu.VMEM((4, 2, size, lanes), jnp.float32),
            pltpu.VMEM((4, 2 * size, lanes), jnp.bfloat16),
            pltpu.VMEM((4, 2, size, lanes), jnp.float32),
        ],
        compiler_params=params(),
        cost_estimate=pl.CostEstimate(flops=9_000_000_000, bytes_accessed=22 << 20, transcendentals=0),
        name="middle",
    )(weights, got, counts, cols, rows)


def turn_rows(got_ref, wide, group, frames, members, first_row, first_lane):
    owners = got_ref.shape[0]
    piece = got_ref[:, first_row : first_row + 16, group * frames : (group + 1) * frames]
    turned = jnp.swapaxes(piece.astype(jnp.float32), 0, 1).astype(jnp.bfloat16)
    for member in range(members):
        for part in range(2):
            at = (2 * part + group) * owners
            for row in range(2):
                lane = first_lane + row * frames
                wide[member, at : at + owners, lane : lane + frames] = turned[4 * member + 2 * part + row]


def early_kernel(got_ref, cols_ref, out_ref, wide):
    member = pl.program_id(0)
    frames = got_ref.shape[2] // 2

    @pl.when(member == 0)
    def _():
        for half in range(2):
            for group in range(2):
                turn_rows(got_ref, wide, group, frames, 4, 16 * half, 2 * half * frames)

    for part in range(2):
        out_ref[0, part] = dot(cols_ref[0, part], wide[member]).astype(jnp.bfloat16)


def early_part(got, cols):
    owners, rows, lanes = got.shape
    size = cols.shape[2]
    return pl.pallas_call(
        early_kernel,
        grid=(4,),
        in_specs=[
            pl.BlockSpec(got.shape, lambda t: (0, 0, 0)),
            pl.BlockSpec((1, 2, size, size), lambda t: (t, 0, 0, 0)),
        ],
        out_specs=pl.BlockSpec((1, 2, size, 2 * lanes), lambda t: (t, 0, 0, 0)),
        out_shape=jax.ShapeDtypeStruct((4, 2, size, 2 * lanes), jnp.bfloat16),
        scratch_shapes=[pltpu.VMEM((4, size, 2 * lanes), jnp.bfloat16)],
        compiler_params=params(),
        cost_estimate=pl.CostEstimate(flops=4_000_000_000, bytes_accessed=10 << 20, transcendentals=0),
        name="early_part",
    )(got, cols)


def last_kernel(
    place_ref, scales_ref, late_ref, real_cols_ref, imag_cols_ref, real_part_ref, imag_part_ref, zb_ref,
    wave_ref, amp_ref, *rest,
):
    out_refs, (wide, field, sum_amp, sum_phase) = rest[:-4], rest[-4:]
    member = pl.program_id(0)
    frames = late_ref.shape[2] // 2
    cells_y, cells_z = amp_ref.shape[1:]

    @pl.when(member == 0)
    def _():
        for group in range(2):
            turn_rows(late_ref, wide, group, frames, 4, 0, 0)
        sum_amp[...] = jnp.zeros_like(sum_amp)
        sum_phase[...] = jnp.zeros_like(sum_phase)

    columns = wide[member]
    real = (dot(real_cols_ref[0, 0], columns) + real_part_ref[0, 0].astype(jnp.float32)).astype(jnp.bfloat16)
    imag = (dot(imag_cols_ref[0, 0], columns) + imag_part_ref[0, 0].astype(jnp.float32)).astype(jnp.bfloat16)
    for row in range(2):
        lane = slice(row * frames, (row + 1) * frames)
        field[row, :, 0:frames] = real[:, lane]
        field[row, :, frames : 2 * frames] = imag[:, lane]
    scale = scales_ref[member]
    tile = 256

    def body(step, carry):
        at = pl.ds(pl.multiple_of(step * tile, tile), tile)
        for row in range(2):
            both = dot(field[row, at, :], zb_ref[0])
            back_real, back_imag = both[:, 0:cells_z], both[:, cells_z : 2 * cells_z]
            wave_real = wave_ref[0, row, at, 0:cells_z].astype(jnp.float32)
            wave_imag = wave_ref[0, row, at, cells_z : 2 * cells_z].astype(jnp.float32)
            sum_amp[row, at, :] += back_real * wave_real - back_imag * wave_imag
            sum_phase[row, at, :] += scale * (back_real * wave_imag + back_imag * wave_real)
        return carry

    lax.fori_loop(0, cells_y // tile, body, 0)

    @pl.when(member == 3)
    def _():
        def close(step, carry):
            at = pl.ds(pl.multiple_of(step * tile, tile), tile)
            for row in range(2):
                out_ref, place = (out_refs[0], row) if len(out_refs) == 1 else (out_refs[row], 0)
                total = sum_amp[row, at, :] / amp_ref[row, at, :].astype(jnp.float32)
                out_ref[place, 0, at, :] = total.astype(jnp.bfloat16)
                out_ref[place, 1, at, :] = sum_phase[row, at, :].astype(jnp.bfloat16)
            return carry

        lax.fori_loop(0, cells_y // tile, close, 0)


def last(place, scales, late, early, cols, zb, wave, amp, half, pieces):
    _, cells_y, cells_z = amp.shape
    owners, _, lanes = late.shape
    size = cols.shape[2]

    def of_part(part, at):
        return lambda t, *_: (t, part, 0, at)

    return pl.pallas_call(
        last_kernel,
        grid_spec=pltpu.PrefetchScalarGridSpec(
            num_scalar_prefetch=2,
            grid=(4,),
            in_specs=[
                pl.BlockSpec((owners, 16, lanes), lambda t, *_: (0, 0, 0)),
                pl.BlockSpec((1, 1, size, size), of_part(0, 1)),
                pl.BlockSpec((1, 1, size, size), of_part(1, 1)),
                pl.BlockSpec((1, 1, size, lanes), of_part(0, half)),
                pl.BlockSpec((1, 1, size, lanes), of_part(1, half)),
                pl.BlockSpec((1,) + zb.shape[1:], lambda t, *_: (t, 0, 0)),
                pl.BlockSpec((1, 2, cells_y, 2 * cells_z), lambda t, *_: (t, half, 0, 0)),
                pl.BlockSpec((2, cells_y, cells_z), lambda t, p, *_: (2 * p[0] + half, 0, 0)),
            ],
            out_specs=[pl.BlockSpec((2 // pieces, 2, cells_y, cells_z), lambda t, *_: (0, 0, 0, 0))] * pieces,
            scratch_shapes=[
                pltpu.VMEM((4, size, lanes), jnp.bfloat16),
                pltpu.VMEM((2, cells_y, lanes), jnp.bfloat16),
                pltpu.VMEM((2, cells_y, cells_z), jnp.float32),
                pltpu.VMEM((2, cells_y, cells_z), jnp.float32),
            ],
        ),
        out_shape=[jax.ShapeDtypeStruct((2 // pieces, 2, cells_y, cells_z), jnp.bfloat16)] * pieces,
        compiler_params=params(),
        cost_estimate=pl.CostEstimate(flops=4_000_000_000, bytes_accessed=16 << 20, transcendentals=0),
        name="last",
    )(place, scales, late, cols, cols, early, early, zb, wave, amp)


def finish_kernel(place_ref, bragg_ref, sums_ref, amp_ref, disp_ref, *rest):
    new_amp_ref, new_disp_ref = rest[-2:]
    new_amp_ref[0] = amp_ref[0].astype(jnp.float32) - step_size * sums_ref[0, 0].astype(jnp.float32)
    sum_phase = sums_ref[0, 1].astype(jnp.float32)
    for axis in range(3):
        new_disp_ref[axis, 0] = (
            disp_ref[axis, 0].astype(jnp.float32) + (step_size * bragg_ref[axis]) * sum_phase
        ).astype(jnp.bfloat16)


def finish(place, bragg, sums, amp, disp, earlier, first_row, other):
    rows = sums.shape[0]
    _, cells_y, cells_z = amp.shape

    def row(t, p):
        half = 1 - p[0] if other else p[0]
        return 4 * half + first_row + t

    amp_spec = pl.BlockSpec((1, cells_y, cells_z), lambda t, p, *_: (row(t, p), 0, 0))
    disp_spec = pl.BlockSpec((3, 1, cells_y, cells_z), lambda t, p, *_: (0, row(t, p), 0, 0))
    kept = [] if earlier is None else list(earlier)
    return pl.pallas_call(
        finish_kernel,
        grid_spec=pltpu.PrefetchScalarGridSpec(
            num_scalar_prefetch=2,
            grid=(rows,),
            in_specs=[
                pl.BlockSpec((1, 2, cells_y, cells_z), lambda t, *_: (t, 0, 0, 0)),
                amp_spec,
                disp_spec,
            ]
            + [pl.BlockSpec(memory_space=pl.ANY)] * len(kept),
            out_specs=[amp_spec, disp_spec],
        ),
        out_shape=[
            jax.ShapeDtypeStruct(amp.shape, jnp.float32),
            jax.ShapeDtypeStruct(disp.shape, jnp.bfloat16),
        ],
        input_output_aliases={} if earlier is None else {5: 0, 6: 1},
        compiler_params=params(small_limit),
        cost_estimate=pl.CostEstimate(flops=10_000_000, bytes_accessed=(3 << 20) * rows, transcendentals=0),
        name="finish",
    )(place, bragg, sums, amp, disp, *kept)


def exchange(blocks):
    return lax.all_to_all(blocks, both_axes, split_axis=0, concat_axis=0, tiled=True)


def swap(values):
    return lax.ppermute(values, "spec", [(0, 1), (1, 0)])


def nothing(*refs):
    pass


def after(values, *others):
    anywhere = pl.BlockSpec(memory_space=pl.ANY)
    return pl.pallas_call(
        nothing,
        in_specs=[anywhere] * (1 + len(others)),
        out_specs=anywhere,
        out_shape=jax.ShapeDtypeStruct(values.shape, values.dtype),
        input_output_aliases={0: 0},
        compiler_params=params(),
        name="after",
    )(values, *others)


def per_device(amplitude, displacement, support, counts, bin_weights, bin_scales, bragg_vector):
    place = lax.axis_index("spec").reshape(1).astype(jnp.int32)
    size, rows_y, frames = counts.shape
    cells_z = amplitude.shape[2]
    volume = (place, bragg_vector, bin_scales, displacement, amplitude, support)
    section, blocks = first_half(*volume, size, frames)
    sent_early = exchange(blocks)
    rows = row_matrices(bin_scales, size)
    wave = waves(*volume)
    sent_late = exchange(after(second_half(section, rows), sent_early, wave))
    cols, zb = column_matrices(bin_scales, size, cells_z, frames)
    mine = lax.dynamic_slice_in_dim(counts, place[0] * (rows_y // 2), rows_y // 2, axis=1)
    mine = mine.reshape(size, rows_y // 2 * frames)
    early_counts, late_counts = mine[:, 0 : 2 * frames], mine[:, 2 * frames : 4 * frames]
    (early,) = middle(bin_weights, sent_early, early_counts, cols, rows, False)
    early = exchange(after(early, sent_late))
    parts = middle(bin_weights, sent_late, late_counts, cols, rows, True)
    early_sum = early_part(early, cols)
    late = [exchange(after(parts[0], early))]
    late.append(exchange(after(parts[1], early_sum, late[0])))
    sums = []
    for half in range(2):
        parts = last(
            place, bin_scales, late[half], early_sum, cols, zb, wave, amplitude, half, 1 + half
        )
        for number, part in enumerate(parts):
            sums.append((2 * half + number, part, swap(part)))
    outs = None
    for other in (False, True):
        for row, mine, theirs in sums:
            outs = finish(
                place, bragg_vector, theirs if other else mine, amplitude, displacement, outs, row, other
            )
    return tuple(outs)


def solution(mesh):
    in_specs = (
        P("slab", None, None),
        P(None, "slab", None, None),
        P("slab", None, None),
        P(None, "slab", None),
        P(),
        P(),
        P(),
    )
    out_specs = (P("slab", None, None), P(None, "slab", None, None))
    return jax.shard_map(
        per_device, mesh=mesh, in_specs=in_specs, out_specs=out_specs, check_vma=False
    )
```

```python
import functools
import math

import jax
import jax.numpy as jnp
from jax import lax
from jax.experimental import pallas as pl
from jax.experimental.pallas import tpu as pltpu
from jax.sharding import PartitionSpec as P

step_size = 0.5
both_axes = ("slab", "spec")
vmem_limit = 62 * 1024 * 1024
small_limit = 36 * 1024 * 1024
cos_terms = (
    0.9999992117703129, -19.738980419471183, 64.92865850463387,
    -85.27162830147759, 58.7905066287335, -21.071108461812614,
)
sin_terms = (
    6.283184916984337, -41.34158926418227, 81.59994386457431,
    -76.61447586037943, 41.342889429509576, -12.4712447471884,
)


wave_cos_terms = (
    0.9999590619701949, -19.73094403547976, 64.67145824268955,
    -82.39085380484792, 45.6210638400798,
)
wave_sin_terms = (
    6.283161153735962, -41.33683281238831, 81.44771611530231,
    -74.90944720114622, 33.548361462485595,
)


def cos_sin_turns(turns, cos_series=cos_terms, sin_series=sin_terms):
    rest = turns - jnp.floor(turns + 0.5)
    square = rest * rest
    cosine = jnp.full_like(square, cos_series[-1])
    sine = jnp.full_like(square, sin_series[-1])
    for level in range(len(cos_series) - 2, -1, -1):
        cosine = cosine * square + cos_series[level]
        sine = sine * square + sin_series[level]
    return cosine, sine * rest


def chirp_parts(out_index, in_index, count_out, count_in, bin_scale):
    product = (out_index - count_out // 2) * (in_index - count_in // 2)
    fraction = (product & (count_in - 1)).astype(jnp.float32) * (1.0 / count_in)
    excess = (bin_scale - 1.0) * (product.astype(jnp.float32) * (1.0 / count_in))
    cosine, sine = cos_sin_turns(fraction + excess)
    normalizer = 1.0 / math.sqrt(count_in)
    return cosine * normalizer, sine * -normalizer


def iota(shape, dim):
    return lax.broadcasted_iota(jnp.int32, shape, dim)


def dot(a, b):
    return jnp.dot(a, b, preferred_element_type=jnp.float32)


def params(limit=vmem_limit):
    return pltpu.CompilerParams(vmem_limit_bytes=limit)


def small_table(index, stride, others, size, bin_scale):
    product = stride * index * others
    fraction = (product & (size - 1)).astype(jnp.float32) * (1.0 / size)
    excess = (bin_scale - 1.0) * (product.astype(jnp.float32) * (1.0 / size))
    cosine, sine = cos_sin_turns(fraction + excess)
    return cosine, -sine


def fill_tables(big_real, big_imag, lane_index, size, bin_scale):
    others = lane_index - size // 2
    wide = (size // 8, size)
    real, imag = small_table(iota(wide, 0) - size // 16, 8, jnp.broadcast_to(others, wide), size, bin_scale)
    normalizer = 1.0 / math.sqrt(size)
    big_real[...] = real * normalizer
    big_imag[...] = imag * normalizer
    narrow = (8, size)
    return small_table(iota(narrow, 0), 1, jnp.broadcast_to(others, narrow), size, bin_scale)


def table_rows(big_real, big_imag, small, step):
    real = jnp.broadcast_to(big_real[pl.ds(step, 1), :], small[0].shape)
    imag = jnp.broadcast_to(big_imag[pl.ds(step, 1), :], small[0].shape)
    return real * small[0] - imag * small[1], real * small[1] + imag * small[0]


def fill_z(zf_ref, member, bin_scale, cells_z, frames):
    real, imag = chirp_parts(
        iota((cells_z, frames), 1), iota((cells_z, frames), 0), frames, cells_z, bin_scale
    )
    zf_ref[member, 0:cells_z, 0:frames] = real.astype(jnp.bfloat16)
    zf_ref[member, 0:cells_z, frames : 2 * frames] = imag.astype(jnp.bfloat16)
    zf_ref[member, cells_z : 2 * cells_z, 0:frames] = (-imag).astype(jnp.bfloat16)
    zf_ref[member, cells_z : 2 * cells_z, frames : 2 * frames] = real.astype(jnp.bfloat16)


def row_matrices_kernel(scales_ref, rows_ref, big_real, big_imag, *, size):
    bin_scale = scales_ref[pl.program_id(0)]
    small = fill_tables(big_real, big_imag, iota((1, size), 1), size, bin_scale)
    low = (iota((8, size), 0) & 2) == 0

    def body(step, carry):
        halves = [[[], []], [[], []]]
        for sub in range(2):
            real, imag = table_rows(big_real, big_imag, small, 2 * step + sub)
            for column, (first, second) in enumerate(((real, imag), (-imag, real))):
                halves[0][column].append(jnp.where(low, first, pltpu.roll(second, 2, 0)))
                halves[1][column].append(jnp.where(low, pltpu.roll(first, 6, 0), second))
        at = pl.ds(pl.multiple_of(16 * step, 16), 16)
        for half in range(2):
            for column in range(2):
                rows_ref[0, half, at, column * size : (column + 1) * size] = jnp.concatenate(
                    halves[half][column], axis=0
                ).astype(jnp.bfloat16)
        return carry

    lax.fori_loop(0, size // 16, body, 0)


def row_matrices(bin_scales, size):
    bins = bin_scales.shape[0]
    return pl.pallas_call(
        functools.partial(row_matrices_kernel, size=size),
        grid=(bins,),
        in_specs=[pl.BlockSpec(memory_space=pltpu.SMEM)],
        out_specs=pl.BlockSpec((1, 2, size, 2 * size), lambda b: (b, 0, 0, 0)),
        out_shape=jax.ShapeDtypeStruct((bins, 2, size, 2 * size), jnp.bfloat16),
        scratch_shapes=[pltpu.VMEM((size // 8, size), jnp.float32)] * 2,
        compiler_params=params(),
        cost_estimate=pl.CostEstimate(flops=4_000_000_000, bytes_accessed=8 << 20, transcendentals=0),
        name="row_matrices",
    )(bin_scales)


def column_matrices_kernel(scales_ref, cols_ref, zb_ref, big_real, big_imag, *, size, cells_z, frames):
    bin_scale = scales_ref[pl.program_id(0)]
    owners = size // 4
    lane = iota((1, size), 1)
    small = fill_tables(big_real, big_imag, 4 * (lane % owners) + lane // owners, size, bin_scale)
    wide = size // 2

    def body(step, carry):
        pairs = [table_rows(big_real, big_imag, small, 2 * step + sub) for sub in range(2)]
        real = jnp.concatenate([pair[0] for pair in pairs], axis=0)
        imag = jnp.concatenate([pair[1] for pair in pairs], axis=0)
        at = pl.ds(pl.multiple_of(16 * step, 16), 16)
        for part, (first, second) in enumerate(((real, -imag), (imag, real))):
            for half in range(2):
                lanes = slice(half * wide, (half + 1) * wide)
                cols_ref[0, part, at, 2 * half * wide : (2 * half + 1) * wide] = first[:, lanes].astype(jnp.bfloat16)
                cols_ref[0, part, at, (2 * half + 1) * wide : (2 * half + 2) * wide] = second[:, lanes].astype(jnp.bfloat16)
        return carry

    lax.fori_loop(0, size // 16, body, 0)
    real, imag = chirp_parts(
        iota((frames, cells_z), 0), iota((frames, cells_z), 1), frames, cells_z, bin_scale
    )
    zb_ref[0, 0:frames, 0:cells_z] = real.astype(jnp.bfloat16)
    zb_ref[0, 0:frames, cells_z : 2 * cells_z] = imag.astype(jnp.bfloat16)
    zb_ref[0, frames : 2 * frames, 0:cells_z] = (-imag).astype(jnp.bfloat16)
    zb_ref[0, frames : 2 * frames, cells_z : 2 * cells_z] = real.astype(jnp.bfloat16)


def column_matrices(bin_scales, size, cells_z, frames):
    bins = bin_scales.shape[0]
    return pl.pallas_call(
        functools.partial(column_matrices_kernel, size=size, cells_z=cells_z, frames=frames),
        grid=(bins,),
        in_specs=[pl.BlockSpec(memory_space=pltpu.SMEM)],
        out_specs=[
            pl.BlockSpec((1, 2, size, 2 * size), lambda b: (b, 0, 0, 0)),
            pl.BlockSpec((1, 2 * frames, 2 * cells_z), lambda b: (b, 0, 0)),
        ],
        out_shape=[
            jax.ShapeDtypeStruct((bins, 2, size, 2 * size), jnp.bfloat16),
            jax.ShapeDtypeStruct((bins, 2 * frames, 2 * cells_z), jnp.bfloat16),
        ],
        scratch_shapes=[pltpu.VMEM((size // 8, size), jnp.float32)] * 2,
        compiler_params=params(),
        cost_estimate=pl.CostEstimate(flops=4_000_000_000, bytes_accessed=8 << 20, transcendentals=0),
        name="column_matrices",
    )(bin_scales)


def pack_owners(values, out_ref, place):
    lanes = out_ref.shape[2]
    tile = 8

    def body(step, carry):
        at = pl.ds(pl.multiple_of(step * 4 * tile, 4 * tile), 4 * tile)
        rows = [values(member, at).reshape(tile // 2, 8, lanes) for member in range(4)]
        low = iota(rows[0].shape, 1) < 4
        even, odd = [], []
        for first, second in ((rows[0], rows[1]), (rows[2], rows[3])):
            even.append(jnp.where(low, first, pltpu.roll(second, 4, 1)))
            odd.append(jnp.where(low, pltpu.roll(first, 4, 1), second))
        even = jnp.concatenate(even, axis=1)
        odd = jnp.concatenate(odd, axis=1)
        both = jnp.stack([even, odd], axis=1).reshape(tile, 16, lanes)
        out_ref[pl.ds(step * tile, tile), pl.ds(place, 16), :] = both.astype(jnp.bfloat16)
        return carry

    lax.fori_loop(0, out_ref.shape[0] // tile, body, 0)


def wave_chunk(bragg_ref, scales_ref, disp_ref, amp_ref, mask_ref, row, at, use):
    phase = (
        bragg_ref[0] * disp_ref[0, row, at, :].astype(jnp.float32)
        + bragg_ref[1] * disp_ref[1, row, at, :].astype(jnp.float32)
        + bragg_ref[2] * disp_ref[2, row, at, :].astype(jnp.float32)
    )
    magnitude = amp_ref[row, at, :].astype(jnp.float32) * mask_ref[row, at, :].astype(jnp.float32)
    for member in range(4):
        cosine, sine = cos_sin_turns(
            (scales_ref[member] * (0.5 / math.pi)) * phase, wave_cos_terms, wave_sin_terms
        )
        use(
            member,
            jnp.concatenate(
                [(magnitude * cosine).astype(jnp.bfloat16), (magnitude * sine).astype(jnp.bfloat16)], axis=1
            ),
        )


def wave_kernel(place_ref, bragg_ref, scales_ref, disp_ref, amp_ref, mask_ref, wave_ref):
    tile = 64

    def body(step, carry):
        at = pl.ds(pl.multiple_of(step * tile, tile), tile)

        def use(member, wave):
            wave_ref[member, 0, at, :] = wave

        wave_chunk(bragg_ref, scales_ref, disp_ref, amp_ref, mask_ref, 0, at, use)
        return carry

    lax.fori_loop(0, amp_ref.shape[1] // tile, body, 0)


def volume_specs(cells_y, cells_z, at_row):
    return [
        pl.BlockSpec((3, 1, cells_y, cells_z), lambda t, p, *_: (0, 4 * p[0] + at_row(t), 0, 0)),
        pl.BlockSpec((1, cells_y, cells_z), lambda t, p, *_: (4 * p[0] + at_row(t), 0, 0)),
        pl.BlockSpec((1, cells_y, cells_z), lambda t, p, *_: (4 * p[0] + at_row(t), 0, 0)),
    ]


def waves(place, bragg, scales, disp, amp, mask):
    _, _, cells_y, cells_z = disp.shape
    return pl.pallas_call(
        wave_kernel,
        grid_spec=pltpu.PrefetchScalarGridSpec(
            num_scalar_prefetch=3,
            grid=(4,),
            in_specs=volume_specs(cells_y, cells_z, lambda t: t),
            out_specs=pl.BlockSpec((4, 1, cells_y, 2 * cells_z), lambda t, *_: (0, t, 0, 0)),
        ),
        out_shape=jax.ShapeDtypeStruct((4, 4, cells_y, 2 * cells_z), jnp.bfloat16),
        compiler_params=params(),
        cost_estimate=pl.CostEstimate(flops=10_000_000_000, bytes_accessed=24 << 20, transcendentals=0),
        name="waves",
    )(place, bragg, scales, disp, amp, mask)


def first_kernel(
    place_ref, bragg_ref, scales_ref, disp_ref, amp_ref, mask_ref,
    section_ref, out_ref, section, held, zf, matrix, big_real, big_imag,
):
    step = pl.program_id(0)
    cells_y, cells_z = amp_ref.shape[1:]
    frames = zf.shape[2] // 2
    size = matrix.shape[0]

    @pl.when(step == 0)
    def _():
        for member in range(4):
            fill_z(zf, member, scales_ref[member], cells_z, frames)

    @pl.when(step < 4)
    def _():
        lanes = pl.ds(pl.multiple_of(step * frames, frames), frames)
        tile = 512

        def body(turn, carry):
            at = pl.ds(pl.multiple_of(turn * tile, tile), tile)
            low = pl.ds(pl.multiple_of(cells_y + turn * tile, tile), tile)

            def use(member, wave):
                both = dot(wave, zf[member]).astype(jnp.bfloat16)
                section[member, at, lanes] = both[:, 0:frames]
                section[member, low, lanes] = both[:, frames : 2 * frames]

            wave_chunk(bragg_ref, scales_ref, disp_ref, amp_ref, mask_ref, 0, at, use)
            return carry

        lax.fori_loop(0, cells_y // tile, body, 0)

    @pl.when(step >= 4)
    def _():
        small = fill_tables(big_real, big_imag, iota((1, size), 1), size, scales_ref[step - 4])
        low = (iota((8, size), 0) & 2) == 0

        def body(turn, carry):
            columns = [[], []]
            for sub in range(8):
                real, imag = table_rows(big_real, big_imag, small, 8 * turn + sub)
                columns[0].append(jnp.where(low, real, pltpu.roll(imag, 2, 0)))
                columns[1].append(jnp.where(low, -imag, pltpu.roll(real, 2, 0)))
            at = pl.ds(pl.multiple_of(64 * turn, 64), 64)
            for column in range(2):
                matrix[at, column * size : (column + 1) * size] = jnp.concatenate(
                    columns[column], axis=0
                ).astype(jnp.bfloat16)
            return carry

        lax.fori_loop(0, size // 64, body, 0)
        section_ref[0] = section[step - 4]
        held[step - 4] = dot(matrix[...], section[step - 4])

    @pl.when(step == 7)
    def _():
        pack_owners(lambda member, at: held[member, at, :], out_ref, 0)


def first_half(place, bragg, scales, disp, amp, mask, size, frames):
    _, _, cells_y, cells_z = disp.shape
    owners = size // 4
    return pl.pallas_call(
        first_kernel,
        grid_spec=pltpu.PrefetchScalarGridSpec(
            num_scalar_prefetch=3,
            grid=(8,),
            in_specs=volume_specs(cells_y, cells_z, lambda t: jnp.minimum(t, 3)),
            out_specs=[
                pl.BlockSpec((1, 2 * cells_y, 4 * frames), lambda t, *_: (jnp.maximum(t - 4, 0), 0, 0)),
                pl.BlockSpec((owners, 16, 4 * frames), lambda t, *_: (0, 0, 0)),
            ],
            scratch_shapes=[
                pltpu.VMEM((4, 2 * cells_y, 4 * frames), jnp.bfloat16),
                pltpu.VMEM((4, size, 4 * frames), jnp.float32),
                pltpu.VMEM((4, 2 * cells_z, 2 * frames), jnp.bfloat16),
                pltpu.VMEM((size, 2 * size), jnp.bfloat16),
                pltpu.VMEM((size // 8, size), jnp.float32),
                pltpu.VMEM((size // 8, size), jnp.float32),
            ],
        ),
        out_shape=[
            jax.ShapeDtypeStruct((4, 2 * cells_y, 4 * frames), jnp.bfloat16),
            jax.ShapeDtypeStruct((owners, 16, 4 * frames), jnp.bfloat16),
        ],
        compiler_params=params(),
        cost_estimate=pl.CostEstimate(flops=9_000_000_000, bytes_accessed=14 << 20, transcendentals=0),
        name="first_half",
    )(place, bragg, scales, disp, amp, mask)


def second_kernel(section_ref, rows_ref, out_ref, held):
    step = pl.program_id(0)
    held[step] = dot(rows_ref[0, 0], section_ref[0])

    @pl.when(step == 3)
    def _():
        pack_owners(lambda member, at: held[member, at, :], out_ref, 0)


def second_half(section, rows):
    size = rows.shape[2]
    lanes = section.shape[2]
    owners = size // 4
    return pl.pallas_call(
        second_kernel,
        grid=(4,),
        in_specs=[
            pl.BlockSpec((1, 2 * size, lanes), lambda t: (t, 0, 0)),
            pl.BlockSpec((1, 1, size, 2 * size), lambda t: (t, 1, 0, 0)),
        ],
        out_specs=pl.BlockSpec((owners, 16, lanes), lambda t: (0, 0, 0)),
        out_shape=jax.ShapeDtypeStruct((owners, 16, lanes), jnp.bfloat16),
        scratch_shapes=[pltpu.VMEM((4, size, lanes), jnp.float32)],
        compiler_params=params(),
        cost_estimate=pl.CostEstimate(flops=3_000_000_000, bytes_accessed=10 << 20, transcendentals=0),
        name="second_half",
    )(section, rows)


def middle_kernel(weights_ref, got_ref, counts_ref, cols_ref, rows_ref, *rest):
    out_refs, (wide, far, back, held) = rest[:-4], rest[-4:]
    step = pl.program_id(0)
    owners = got_ref.shape[0]
    size = far.shape[2]
    frames = got_ref.shape[2] // 4
    lanes = 2 * frames

    @pl.when(step == 0)
    def _():
        for group in range(4):
            piece = got_ref[:, :, group * frames : (group + 1) * frames].astype(jnp.float32)
            turned = jnp.swapaxes(piece, 0, 1).astype(jnp.bfloat16)
            for member in range(4):
                for part in range(2):
                    at = (4 * (group // 2) + 2 * part + group % 2) * owners
                    for row in range(2):
                        wide[member, at : at + owners, row * frames : (row + 1) * frames] = turned[
                            4 * member + 2 * part + row
                        ]

    @pl.when(step < 4)
    def _():
        for part in range(2):
            far[step, part] = dot(cols_ref[0, part], wide[step])

    @pl.when(step == 3)
    def _():
        def body(turn, carry):
            at = pl.ds(pl.multiple_of(turn * 16, 16), 16)
            fields = [(far[member, 0, at, :], far[member, 1, at, :]) for member in range(4)]
            intensity = None
            for member, (real, imag) in enumerate(fields):
                term = weights_ref[member] * (real * real + imag * imag)
                intensity = term if intensity is None else intensity + term
            ratio = 1.0 - jnp.sqrt(counts_ref[at, :].astype(jnp.float32) / jnp.maximum(intensity, 0.5))
            for member, (real, imag) in enumerate(fields):
                factor = weights_ref[member] * ratio
                back[member, at, :] = (factor * real).astype(jnp.bfloat16)
                low = pl.ds(pl.multiple_of(size + turn * 16, 16), 16)
                back[member, low, :] = (-factor * imag).astype(jnp.bfloat16)
            return carry

        lax.fori_loop(0, size // 16, body, 0)

    @pl.when(step >= 4)
    def _():
        for half in range(2):
            held[step - 4, half] = dot(rows_ref[0, half], back[step - 4])

    @pl.when(step == 7)
    def _():
        for half in range(2):
            out_ref, place = (out_refs[0], 16 * half) if len(out_refs) == 1 else (out_refs[half], 0)
            pack_owners(lambda member, at, half=half: held[member, half, at, :], out_ref, place)


def middle(weights, got, counts, cols, rows, split):
    owners, _, lanes4 = got.shape
    size = rows.shape[2]
    lanes = lanes4 // 2
    if split:
        shapes = [(owners, 16, lanes)] * 2
    else:
        shapes = [(owners, 32, lanes)]
    return pl.pallas_call(
        middle_kernel,
        grid=(8,),
        in_specs=[
            pl.BlockSpec(memory_space=pltpu.SMEM),
            pl.BlockSpec(got.shape, lambda t: (0, 0, 0)),
            pl.BlockSpec(counts.shape, lambda t: (0, 0)),
            pl.BlockSpec((1, 2, size, 2 * size), lambda t: (jnp.minimum(t, 3), 0, 0, 0)),
            pl.BlockSpec((1, 2, size, 2 * size), lambda t: (jnp.maximum(t - 4, 0), 0, 0, 0)),
        ],
        out_specs=[pl.BlockSpec(shape, lambda t: (0, 0, 0)) for shape in shapes],
        out_shape=[jax.ShapeDtypeStruct(shape, jnp.bfloat16) for shape in shapes],
        scratch_shapes=[
            pltpu.VMEM((4, 2 * size, lanes), jnp.bfloat16),
            pltpu.VMEM((4, 2, size, lanes), jnp.float32),
            pltpu.VMEM((4, 2 * size, lanes), jnp.bfloat16),
            pltpu.VMEM((4, 2, size, lanes), jnp.float32),
        ],
        compiler_params=params(),
        cost_estimate=pl.CostEstimate(flops=9_000_000_000, bytes_accessed=22 << 20, transcendentals=0),
        name="middle",
    )(weights, got, counts, cols, rows)


def turn_rows(got_ref, wide, group, frames, members, first_row, first_lane):
    owners = got_ref.shape[0]
    piece = got_ref[:, first_row : first_row + 16, group * frames : (group + 1) * frames]
    turned = jnp.swapaxes(piece.astype(jnp.float32), 0, 1).astype(jnp.bfloat16)
    for member in range(members):
        for part in range(2):
            at = (2 * part + group) * owners
            for row in range(2):
                lane = first_lane + row * frames
                wide[member, at : at + owners, lane : lane + frames] = turned[4 * member + 2 * part + row]


def early_kernel(got_ref, cols_ref, out_ref, wide):
    member = pl.program_id(0)
    frames = got_ref.shape[2] // 2

    @pl.when(member == 0)
    def _():
        for half in range(2):
            for group in range(2):
                turn_rows(got_ref, wide, group, frames, 4, 16 * half, 2 * half * frames)

    for part in range(2):
        out_ref[0, part] = dot(cols_ref[0, part], wide[member]).astype(jnp.bfloat16)


def early_part(got, cols):
    owners, rows, lanes = got.shape
    size = cols.shape[2]
    return pl.pallas_call(
        early_kernel,
        grid=(4,),
        in_specs=[
            pl.BlockSpec(got.shape, lambda t: (0, 0, 0)),
            pl.BlockSpec((1, 2, size, size), lambda t: (t, 0, 0, 0)),
        ],
        out_specs=pl.BlockSpec((1, 2, size, 2 * lanes), lambda t: (t, 0, 0, 0)),
        out_shape=jax.ShapeDtypeStruct((4, 2, size, 2 * lanes), jnp.bfloat16),
        scratch_shapes=[pltpu.VMEM((4, size, 2 * lanes), jnp.bfloat16)],
        compiler_params=params(),
        cost_estimate=pl.CostEstimate(flops=4_000_000_000, bytes_accessed=10 << 20, transcendentals=0),
        name="early_part",
    )(got, cols)


def last_kernel(
    place_ref, scales_ref, late_ref, real_cols_ref, imag_cols_ref, real_part_ref, imag_part_ref, zb_ref,
    wave_ref, amp_ref, *rest,
):
    out_refs, (wide, field, sum_amp, sum_phase) = rest[:-4], rest[-4:]
    member = pl.program_id(0)
    frames = late_ref.shape[2] // 2
    cells_y, cells_z = amp_ref.shape[1:]

    @pl.when(member == 0)
    def _():
        for group in range(2):
            turn_rows(late_ref, wide, group, frames, 4, 0, 0)
        sum_amp[...] = jnp.zeros_like(sum_amp)
        sum_phase[...] = jnp.zeros_like(sum_phase)

    columns = wide[member]
    real = (dot(real_cols_ref[0, 0], columns) + real_part_ref[0, 0].astype(jnp.float32)).astype(jnp.bfloat16)
    imag = (dot(imag_cols_ref[0, 0], columns) + imag_part_ref[0, 0].astype(jnp.float32)).astype(jnp.bfloat16)
    for row in range(2):
        lane = slice(row * frames, (row + 1) * frames)
        field[row, :, 0:frames] = real[:, lane]
        field[row, :, frames : 2 * frames] = imag[:, lane]
    scale = scales_ref[member]
    tile = 256

    def body(step, carry):
        at = pl.ds(pl.multiple_of(step * tile, tile), tile)
        for row in range(2):
            both = dot(field[row, at, :], zb_ref[0])
            back_real, back_imag = both[:, 0:cells_z], both[:, cells_z : 2 * cells_z]
            wave_real = wave_ref[0, row, at, 0:cells_z].astype(jnp.float32)
            wave_imag = wave_ref[0, row, at, cells_z : 2 * cells_z].astype(jnp.float32)
            sum_amp[row, at, :] += back_real * wave_real - back_imag * wave_imag
            sum_phase[row, at, :] += scale * (back_real * wave_imag + back_imag * wave_real)
        return carry

    lax.fori_loop(0, cells_y // tile, body, 0)

    @pl.when(member == 3)
    def _():
        def close(step, carry):
            at = pl.ds(pl.multiple_of(step * tile, tile), tile)
            for row in range(2):
                out_ref, place = (out_refs[0], row) if len(out_refs) == 1 else (out_refs[row], 0)
                total = sum_amp[row, at, :] / amp_ref[row, at, :].astype(jnp.float32)
                out_ref[place, 0, at, :] = total.astype(jnp.bfloat16)
                out_ref[place, 1, at, :] = sum_phase[row, at, :].astype(jnp.bfloat16)
            return carry

        lax.fori_loop(0, cells_y // tile, close, 0)


def last(place, scales, late, early, cols, zb, wave, amp, half, pieces):
    _, cells_y, cells_z = amp.shape
    owners, _, lanes = late.shape
    size = cols.shape[2]

    def of_part(part, at):
        return lambda t, *_: (t, part, 0, at)

    return pl.pallas_call(
        last_kernel,
        grid_spec=pltpu.PrefetchScalarGridSpec(
            num_scalar_prefetch=2,
            grid=(4,),
            in_specs=[
                pl.BlockSpec((owners, 16, lanes), lambda t, *_: (0, 0, 0)),
                pl.BlockSpec((1, 1, size, size), of_part(0, 1)),
                pl.BlockSpec((1, 1, size, size), of_part(1, 1)),
                pl.BlockSpec((1, 1, size, lanes), of_part(0, half)),
                pl.BlockSpec((1, 1, size, lanes), of_part(1, half)),
                pl.BlockSpec((1,) + zb.shape[1:], lambda t, *_: (t, 0, 0)),
                pl.BlockSpec((1, 2, cells_y, 2 * cells_z), lambda t, *_: (t, half, 0, 0)),
                pl.BlockSpec((2, cells_y, cells_z), lambda t, p, *_: (2 * p[0] + half, 0, 0)),
            ],
            out_specs=[pl.BlockSpec((2 // pieces, 2, cells_y, cells_z), lambda t, *_: (0, 0, 0, 0))] * pieces,
            scratch_shapes=[
                pltpu.VMEM((4, size, lanes), jnp.bfloat16),
                pltpu.VMEM((2, cells_y, lanes), jnp.bfloat16),
                pltpu.VMEM((2, cells_y, cells_z), jnp.float32),
                pltpu.VMEM((2, cells_y, cells_z), jnp.float32),
            ],
        ),
        out_shape=[jax.ShapeDtypeStruct((2 // pieces, 2, cells_y, cells_z), jnp.bfloat16)] * pieces,
        compiler_params=params(),
        cost_estimate=pl.CostEstimate(flops=4_000_000_000, bytes_accessed=16 << 20, transcendentals=0),
        name="last",
    )(place, scales, late, cols, cols, early, early, zb, wave, amp)


def finish_kernel(place_ref, bragg_ref, sums_ref, amp_ref, disp_ref, *rest):
    new_amp_ref, new_disp_ref = rest[-2:]
    new_amp_ref[0] = amp_ref[0].astype(jnp.float32) - step_size * sums_ref[0, 0].astype(jnp.float32)
    sum_phase = sums_ref[0, 1].astype(jnp.float32)
    for axis in range(3):
        new_disp_ref[axis, 0] = (
            disp_ref[axis, 0].astype(jnp.float32) + (step_size * bragg_ref[axis]) * sum_phase
        ).astype(jnp.bfloat16)


def finish(place, bragg, sums, amp, disp, earlier, first_row, other):
    rows = sums.shape[0]
    _, cells_y, cells_z = amp.shape

    def row(t, p):
        half = 1 - p[0] if other else p[0]
        return 4 * half + first_row + t

    amp_spec = pl.BlockSpec((1, cells_y, cells_z), lambda t, p, *_: (row(t, p), 0, 0))
    disp_spec = pl.BlockSpec((3, 1, cells_y, cells_z), lambda t, p, *_: (0, row(t, p), 0, 0))
    kept = [] if earlier is None else list(earlier)
    return pl.pallas_call(
        finish_kernel,
        grid_spec=pltpu.PrefetchScalarGridSpec(
            num_scalar_prefetch=2,
            grid=(rows,),
            in_specs=[
                pl.BlockSpec((1, 2, cells_y, cells_z), lambda t, *_: (t, 0, 0, 0)),
                amp_spec,
                disp_spec,
            ]
            + [pl.BlockSpec(memory_space=pl.ANY)] * len(kept),
            out_specs=[amp_spec, disp_spec],
        ),
        out_shape=[
            jax.ShapeDtypeStruct(amp.shape, jnp.float32),
            jax.ShapeDtypeStruct(disp.shape, jnp.bfloat16),
        ],
        input_output_aliases={} if earlier is None else {5: 0, 6: 1},
        compiler_params=params(small_limit),
        cost_estimate=pl.CostEstimate(flops=10_000_000, bytes_accessed=(3 << 20) * rows, transcendentals=0),
        name="finish",
    )(place, bragg, sums, amp, disp, *kept)


def exchange(blocks):
    return lax.all_to_all(blocks, both_axes, split_axis=0, concat_axis=0, tiled=True)


def swap(values):
    return lax.ppermute(values, "spec", [(0, 1), (1, 0)])


def nothing(*refs):
    pass


def after(values, *others):
    anywhere = pl.BlockSpec(memory_space=pl.ANY)
    return pl.pallas_call(
        nothing,
        in_specs=[anywhere] * (1 + len(others)),
        out_specs=anywhere,
        out_shape=jax.ShapeDtypeStruct(values.shape, values.dtype),
        input_output_aliases={0: 0},
        compiler_params=params(),
        name="after",
    )(values, *others)


def per_device(amplitude, displacement, support, counts, bin_weights, bin_scales, bragg_vector):
    place = lax.axis_index("spec").reshape(1).astype(jnp.int32)
    size, rows_y, frames = counts.shape
    cells_z = amplitude.shape[2]
    volume = (place, bragg_vector, bin_scales, displacement, amplitude, support)
    section, blocks = first_half(*volume, size, frames)
    sent_early = exchange(blocks)
    rows = row_matrices(bin_scales, size)
    wave = waves(*volume)
    sent_late = exchange(after(second_half(section, rows), sent_early, wave))
    cols, zb = column_matrices(bin_scales, size, cells_z, frames)
    mine = lax.dynamic_slice_in_dim(counts, place[0] * (rows_y // 2), rows_y // 2, axis=1)
    mine = mine.reshape(size, rows_y // 2 * frames)
    early_counts, late_counts = mine[:, 0 : 2 * frames], mine[:, 2 * frames : 4 * frames]
    (early,) = middle(bin_weights, sent_early, early_counts, cols, rows, False)
    early = exchange(after(early, sent_late))
    parts = middle(bin_weights, sent_late, late_counts, cols, rows, True)
    early_sum = early_part(early, cols)
    late = [exchange(after(parts[0], early))]
    late.append(exchange(after(parts[1], early_sum, late[0])))
    sums = []
    for half in range(2):
        parts = last(
            place, bin_scales, late[half], early_sum, cols, zb, wave, amplitude, half, 1 + half
        )
        for number, part in enumerate(parts):
            sums.append((2 * half + number, part, swap(part)))
    outs = None
    for other in (False, True):
        for row, mine, theirs in sums:
            outs = finish(
                place, bragg_vector, theirs if other else mine, amplitude, displacement, outs, row, other
            )
    return tuple(outs)


def solution(mesh):
    in_specs = (
        P("slab", None, None),
        P(None, "slab", None, None),
        P("slab", None, None),
        P(None, "slab", None),
        P(),
        P(),
        P(),
    )
    out_specs = (P("slab", None, None), P(None, "slab", None, None))
    return jax.shard_map(
        per_device, mesh=mesh, in_specs=in_specs, out_specs=out_specs, check_vma=False
    )
```

```python
import functools
import math

import jax
import jax.numpy as jnp
from jax import lax
from jax.experimental import pallas as pl
from jax.experimental.pallas import tpu as pltpu
from jax.sharding import PartitionSpec as P

step_size = 0.5
both_axes = ("slab", "spec")
vmem_limit = 62 * 1024 * 1024
small_limit = 36 * 1024 * 1024
cos_terms = (
    0.9999992117703129, -19.738980419471183, 64.92865850463387,
    -85.27162830147759, 58.7905066287335, -21.071108461812614,
)
sin_terms = (
    6.283184916984337, -41.34158926418227, 81.59994386457431,
    -76.61447586037943, 41.342889429509576, -12.4712447471884,
)


wave_cos_terms = (
    0.9999590619701949, -19.73094403547976, 64.67145824268955,
    -82.39085380484792, 45.6210638400798,
)
wave_sin_terms = (
    6.283161153735962, -41.33683281238831, 81.44771611530231,
    -74.90944720114622, 33.548361462485595,
)


def cos_sin_turns(turns, cos_series=cos_terms, sin_series=sin_terms):
    rest = turns - jnp.round(turns)
    square = rest * rest
    cosine = jnp.full_like(square, cos_series[-1])
    sine = jnp.full_like(square, sin_series[-1])
    for level in range(len(cos_series) - 2, -1, -1):
        cosine = cosine * square + cos_series[level]
        sine = sine * square + sin_series[level]
    return cosine, sine * rest


def chirp_parts(out_index, in_index, count_out, count_in, bin_scale):
    product = (out_index - count_out // 2) * (in_index - count_in // 2)
    fraction = (product & (count_in - 1)).astype(jnp.float32) * (1.0 / count_in)
    excess = (bin_scale - 1.0) * (product.astype(jnp.float32) * (1.0 / count_in))
    cosine, sine = cos_sin_turns(fraction + excess)
    normalizer = 1.0 / math.sqrt(count_in)
    return cosine * normalizer, sine * -normalizer


def iota(shape, dim):
    return lax.broadcasted_iota(jnp.int32, shape, dim)


def dot(a, b):
    return jnp.dot(a, b, preferred_element_type=jnp.float32)


def params(limit=vmem_limit):
    return pltpu.CompilerParams(vmem_limit_bytes=limit)


def small_table(index, stride, others, size, bin_scale):
    product = stride * index * others
    fraction = (product & (size - 1)).astype(jnp.float32) * (1.0 / size)
    excess = (bin_scale - 1.0) * (product.astype(jnp.float32) * (1.0 / size))
    cosine, sine = cos_sin_turns(fraction + excess)
    return cosine, -sine


def fill_tables(big_real, big_imag, lane_index, size, bin_scale):
    others = lane_index - size // 2
    wide = (size // 8, size)
    real, imag = small_table(iota(wide, 0) - size // 16, 8, jnp.broadcast_to(others, wide), size, bin_scale)
    normalizer = 1.0 / math.sqrt(size)
    big_real[...] = real * normalizer
    big_imag[...] = imag * normalizer
    narrow = (8, size)
    return small_table(iota(narrow, 0), 1, jnp.broadcast_to(others, narrow), size, bin_scale)


def table_rows(big_real, big_imag, small, step):
    real = jnp.broadcast_to(big_real[pl.ds(step, 1), :], small[0].shape)
    imag = jnp.broadcast_to(big_imag[pl.ds(step, 1), :], small[0].shape)
    return real * small[0] - imag * small[1], real * small[1] + imag * small[0]


def fill_z(zf_ref, member, bin_scale, cells_z, frames):
    real, imag = chirp_parts(
        iota((cells_z, frames), 1), iota((cells_z, frames), 0), frames, cells_z, bin_scale
    )
    zf_ref[member, 0:cells_z, 0:frames] = real.astype(jnp.bfloat16)
    zf_ref[member, 0:cells_z, frames : 2 * frames] = imag.astype(jnp.bfloat16)
    zf_ref[member, cells_z : 2 * cells_z, 0:frames] = (-imag).astype(jnp.bfloat16)
    zf_ref[member, cells_z : 2 * cells_z, frames : 2 * frames] = real.astype(jnp.bfloat16)


def row_matrices_kernel(scales_ref, rows_ref, big_real, big_imag, *, size):
    bin_scale = scales_ref[pl.program_id(0)]
    small = fill_tables(big_real, big_imag, iota((1, size), 1), size, bin_scale)
    low = (iota((8, size), 0) & 2) == 0

    def body(step, carry):
        halves = [[[], []], [[], []]]
        for sub in range(2):
            real, imag = table_rows(big_real, big_imag, small, 2 * step + sub)
            for column, (first, second) in enumerate(((real, imag), (-imag, real))):
                halves[0][column].append(jnp.where(low, first, pltpu.roll(second, 2, 0)))
                halves[1][column].append(jnp.where(low, pltpu.roll(first, 6, 0), second))
        at = pl.ds(pl.multiple_of(16 * step, 16), 16)
        for half in range(2):
            for column in range(2):
                rows_ref[0, half, at, column * size : (column + 1) * size] = jnp.concatenate(
                    halves[half][column], axis=0
                ).astype(jnp.bfloat16)
        return carry

    lax.fori_loop(0, size // 16, body, 0)


def row_matrices(bin_scales, size):
    bins = bin_scales.shape[0]
    return pl.pallas_call(
        functools.partial(row_matrices_kernel, size=size),
        grid=(bins,),
        in_specs=[pl.BlockSpec(memory_space=pltpu.SMEM)],
        out_specs=pl.BlockSpec((1, 2, size, 2 * size), lambda b: (b, 0, 0, 0)),
        out_shape=jax.ShapeDtypeStruct((bins, 2, size, 2 * size), jnp.bfloat16),
        scratch_shapes=[pltpu.VMEM((size // 8, size), jnp.float32)] * 2,
        compiler_params=params(),
        cost_estimate=pl.CostEstimate(flops=4_000_000_000, bytes_accessed=8 << 20, transcendentals=0),
        name="row_matrices",
    )(bin_scales)


def column_matrices_kernel(scales_ref, cols_ref, zb_ref, big_real, big_imag, *, size, cells_z, frames):
    bin_scale = scales_ref[pl.program_id(0)]
    owners = size // 4
    lane = iota((1, size), 1)
    small = fill_tables(big_real, big_imag, 4 * (lane % owners) + lane // owners, size, bin_scale)
    wide = size // 2

    def body(step, carry):
        pairs = [table_rows(big_real, big_imag, small, 2 * step + sub) for sub in range(2)]
        real = jnp.concatenate([pair[0] for pair in pairs], axis=0)
        imag = jnp.concatenate([pair[1] for pair in pairs], axis=0)
        at = pl.ds(pl.multiple_of(16 * step, 16), 16)
        for part, (first, second) in enumerate(((real, -imag), (imag, real))):
            for half in range(2):
                lanes = slice(half * wide, (half + 1) * wide)
                cols_ref[0, part, at, 2 * half * wide : (2 * half + 1) * wide] = first[:, lanes].astype(jnp.bfloat16)
                cols_ref[0, part, at, (2 * half + 1) * wide : (2 * half + 2) * wide] = second[:, lanes].astype(jnp.bfloat16)
        return carry

    lax.fori_loop(0, size // 16, body, 0)
    real, imag = chirp_parts(
        iota((frames, cells_z), 0), iota((frames, cells_z), 1), frames, cells_z, bin_scale
    )
    zb_ref[0, 0:frames, 0:cells_z] = real.astype(jnp.bfloat16)
    zb_ref[0, 0:frames, cells_z : 2 * cells_z] = imag.astype(jnp.bfloat16)
    zb_ref[0, frames : 2 * frames, 0:cells_z] = (-imag).astype(jnp.bfloat16)
    zb_ref[0, frames : 2 * frames, cells_z : 2 * cells_z] = real.astype(jnp.bfloat16)


def column_matrices(bin_scales, size, cells_z, frames):
    bins = bin_scales.shape[0]
    return pl.pallas_call(
        functools.partial(column_matrices_kernel, size=size, cells_z=cells_z, frames=frames),
        grid=(bins,),
        in_specs=[pl.BlockSpec(memory_space=pltpu.SMEM)],
        out_specs=[
            pl.BlockSpec((1, 2, size, 2 * size), lambda b: (b, 0, 0, 0)),
            pl.BlockSpec((1, 2 * frames, 2 * cells_z), lambda b: (b, 0, 0)),
        ],
        out_shape=[
            jax.ShapeDtypeStruct((bins, 2, size, 2 * size), jnp.bfloat16),
            jax.ShapeDtypeStruct((bins, 2 * frames, 2 * cells_z), jnp.bfloat16),
        ],
        scratch_shapes=[pltpu.VMEM((size // 8, size), jnp.float32)] * 2,
        compiler_params=params(),
        cost_estimate=pl.CostEstimate(flops=4_000_000_000, bytes_accessed=8 << 20, transcendentals=0),
        name="column_matrices",
    )(bin_scales)


def pack_owners(values, out_ref, place):
    lanes = out_ref.shape[2]
    tile = 8

    def body(step, carry):
        at = pl.ds(pl.multiple_of(step * 4 * tile, 4 * tile), 4 * tile)
        rows = [values(member, at).reshape(tile // 2, 8, lanes) for member in range(4)]
        low = iota(rows[0].shape, 1) < 4
        even, odd = [], []
        for first, second in ((rows[0], rows[1]), (rows[2], rows[3])):
            even.append(jnp.where(low, first, pltpu.roll(second, 4, 1)))
            odd.append(jnp.where(low, pltpu.roll(first, 4, 1), second))
        even = jnp.concatenate(even, axis=1)
        odd = jnp.concatenate(odd, axis=1)
        both = jnp.stack([even, odd], axis=1).reshape(tile, 16, lanes)
        out_ref[pl.ds(step * tile, tile), pl.ds(place, 16), :] = both.astype(jnp.bfloat16)
        return carry

    lax.fori_loop(0, out_ref.shape[0] // tile, body, 0)


def wave_chunk(bragg_ref, scales_ref, disp_ref, amp_ref, mask_ref, row, at, use):
    phase = (
        bragg_ref[0] * disp_ref[0, row, at, :].astype(jnp.float32)
        + bragg_ref[1] * disp_ref[1, row, at, :].astype(jnp.float32)
        + bragg_ref[2] * disp_ref[2, row, at, :].astype(jnp.float32)
    )
    magnitude = amp_ref[row, at, :].astype(jnp.float32) * mask_ref[row, at, :].astype(jnp.float32)
    for member in range(4):
        cosine, sine = cos_sin_turns(
            (scales_ref[member] * (0.5 / math.pi)) * phase, wave_cos_terms, wave_sin_terms
        )
        use(
            member,
            jnp.concatenate(
                [(magnitude * cosine).astype(jnp.bfloat16), (magnitude * sine).astype(jnp.bfloat16)], axis=1
            ),
        )


def wave_kernel(place_ref, bragg_ref, scales_ref, disp_ref, amp_ref, mask_ref, wave_ref):
    tile = 64

    def body(step, carry):
        at = pl.ds(pl.multiple_of(step * tile, tile), tile)

        def use(member, wave):
            wave_ref[member, 0, at, :] = wave

        wave_chunk(bragg_ref, scales_ref, disp_ref, amp_ref, mask_ref, 0, at, use)
        return carry

    lax.fori_loop(0, amp_ref.shape[1] // tile, body, 0)


def volume_specs(cells_y, cells_z, at_row):
    return [
        pl.BlockSpec((3, 1, cells_y, cells_z), lambda t, p, *_: (0, 4 * p[0] + at_row(t), 0, 0)),
        pl.BlockSpec((1, cells_y, cells_z), lambda t, p, *_: (4 * p[0] + at_row(t), 0, 0)),
        pl.BlockSpec((1, cells_y, cells_z), lambda t, p, *_: (4 * p[0] + at_row(t), 0, 0)),
    ]


def waves(place, bragg, scales, disp, amp, mask):
    _, _, cells_y, cells_z = disp.shape
    return pl.pallas_call(
        wave_kernel,
        grid_spec=pltpu.PrefetchScalarGridSpec(
            num_scalar_prefetch=3,
            grid=(4,),
            in_specs=volume_specs(cells_y, cells_z, lambda t: t),
            out_specs=pl.BlockSpec((4, 1, cells_y, 2 * cells_z), lambda t, *_: (0, t, 0, 0)),
        ),
        out_shape=jax.ShapeDtypeStruct((4, 4, cells_y, 2 * cells_z), jnp.bfloat16),
        compiler_params=params(),
        cost_estimate=pl.CostEstimate(flops=10_000_000_000, bytes_accessed=24 << 20, transcendentals=0),
        name="waves",
    )(place, bragg, scales, disp, amp, mask)


def first_kernel(
    place_ref, bragg_ref, scales_ref, disp_ref, amp_ref, mask_ref,
    section_ref, out_ref, section, held, zf, matrix, big_real, big_imag,
):
    step = pl.program_id(0)
    cells_y, cells_z = amp_ref.shape[1:]
    frames = zf.shape[2] // 2
    size = matrix.shape[0]

    @pl.when(step == 0)
    def _():
        for member in range(4):
            fill_z(zf, member, scales_ref[member], cells_z, frames)

    @pl.when(step < 4)
    def _():
        lanes = pl.ds(pl.multiple_of(step * frames, frames), frames)
        tile = cells_y // 2
        for turn in range(2):
            at = slice(turn * tile, (turn + 1) * tile)
            low = slice(cells_y + turn * tile, cells_y + (turn + 1) * tile)

            def use(member, wave, at=at, low=low):
                both = dot(wave, zf[member]).astype(jnp.bfloat16)
                section[member, at, lanes] = both[:, 0:frames]
                section[member, low, lanes] = both[:, frames : 2 * frames]

            wave_chunk(bragg_ref, scales_ref, disp_ref, amp_ref, mask_ref, 0, at, use)

    @pl.when(step >= 4)
    def _():
        small = fill_tables(big_real, big_imag, iota((1, size), 1), size, scales_ref[step - 4])
        low = (iota((8, size), 0) & 2) == 0

        section_ref[0] = section[step - 4]
        chunk = size // 2
        for piece in range(2):
            columns = [[], []]
            for turn in range(piece * chunk // 8, (piece + 1) * chunk // 8):
                real, imag = table_rows(big_real, big_imag, small, turn)
                columns[0].append(jnp.where(low, real, pltpu.roll(imag, 2, 0)))
                columns[1].append(jnp.where(low, -imag, pltpu.roll(real, 2, 0)))
            both = [jnp.concatenate(column, axis=0).astype(jnp.bfloat16) for column in columns]
            held[step - 4, piece * chunk : (piece + 1) * chunk, :] = dot(
                jnp.concatenate(both, axis=1), section[step - 4]
            )

    @pl.when(step == 7)
    def _():
        pack_owners(lambda member, at: held[member, at, :], out_ref, 0)


def first_half(place, bragg, scales, disp, amp, mask, size, frames):
    _, _, cells_y, cells_z = disp.shape
    owners = size // 4
    return pl.pallas_call(
        first_kernel,
        grid_spec=pltpu.PrefetchScalarGridSpec(
            num_scalar_prefetch=3,
            grid=(8,),
            in_specs=volume_specs(cells_y, cells_z, lambda t: jnp.minimum(t, 3)),
            out_specs=[
                pl.BlockSpec((1, 2 * cells_y, 4 * frames), lambda t, *_: (jnp.maximum(t - 4, 0), 0, 0)),
                pl.BlockSpec((owners, 16, 4 * frames), lambda t, *_: (0, 0, 0)),
            ],
            scratch_shapes=[
                pltpu.VMEM((4, 2 * cells_y, 4 * frames), jnp.bfloat16),
                pltpu.VMEM((4, size, 4 * frames), jnp.float32),
                pltpu.VMEM((4, 2 * cells_z, 2 * frames), jnp.bfloat16),
                pltpu.VMEM((size, 2 * size), jnp.bfloat16),
                pltpu.VMEM((size // 8, size), jnp.float32),
                pltpu.VMEM((size // 8, size), jnp.float32),
            ],
        ),
        out_shape=[
            jax.ShapeDtypeStruct((4, 2 * cells_y, 4 * frames), jnp.bfloat16),
            jax.ShapeDtypeStruct((owners, 16, 4 * frames), jnp.bfloat16),
        ],
        compiler_params=params(),
        cost_estimate=pl.CostEstimate(flops=9_000_000_000, bytes_accessed=14 << 20, transcendentals=0),
        name="first_half",
    )(place, bragg, scales, disp, amp, mask)


def second_kernel(section_ref, rows_ref, out_ref, held):
    step = pl.program_id(0)
    held[step] = dot(rows_ref[0, 0], section_ref[0])

    @pl.when(step == 3)
    def _():
        pack_owners(lambda member, at: held[member, at, :], out_ref, 0)


def second_half(section, rows):
    size = rows.shape[2]
    lanes = section.shape[2]
    owners = size // 4
    return pl.pallas_call(
        second_kernel,
        grid=(4,),
        in_specs=[
            pl.BlockSpec((1, 2 * size, lanes), lambda t: (t, 0, 0)),
            pl.BlockSpec((1, 1, size, 2 * size), lambda t: (t, 1, 0, 0)),
        ],
        out_specs=pl.BlockSpec((owners, 16, lanes), lambda t: (0, 0, 0)),
        out_shape=jax.ShapeDtypeStruct((owners, 16, lanes), jnp.bfloat16),
        scratch_shapes=[pltpu.VMEM((4, size, lanes), jnp.float32)],
        compiler_params=params(),
        cost_estimate=pl.CostEstimate(flops=3_000_000_000, bytes_accessed=10 << 20, transcendentals=0),
        name="second_half",
    )(section, rows)


def middle_kernel(weights_ref, got_ref, counts_ref, cols_ref, rows_ref, *rest):
    out_refs, (wide, far, back, held) = rest[:-4], rest[-4:]
    step = pl.program_id(0)
    owners = got_ref.shape[0]
    size = far.shape[2]
    frames = got_ref.shape[2] // 4
    lanes = 2 * frames

    @pl.when(step == 0)
    def _():
        for group in range(4):
            piece = got_ref[:, :, group * frames : (group + 1) * frames].astype(jnp.float32)
            turned = jnp.swapaxes(piece, 0, 1).astype(jnp.bfloat16)
            for member in range(4):
                for part in range(2):
                    at = (4 * (group // 2) + 2 * part + group % 2) * owners
                    for row in range(2):
                        wide[member, at : at + owners, row * frames : (row + 1) * frames] = turned[
                            4 * member + 2 * part + row
                        ]

    @pl.when(step < 4)
    def _():
        for part in range(2):
            far[step, part] = dot(cols_ref[0, part], wide[step])

    @pl.when(step == 3)
    def _():
        def body(turn, carry):
            at = pl.ds(pl.multiple_of(turn * 16, 16), 16)
            fields = [(far[member, 0, at, :], far[member, 1, at, :]) for member in range(4)]
            intensity = None
            for member, (real, imag) in enumerate(fields):
                term = weights_ref[member] * (real * real + imag * imag)
                intensity = term if intensity is None else intensity + term
            ratio = 1.0 - jnp.sqrt(counts_ref[at, :].astype(jnp.float32) / jnp.maximum(intensity, 0.5))
            for member, (real, imag) in enumerate(fields):
                factor = weights_ref[member] * ratio
                back[member, at, :] = (factor * real).astype(jnp.bfloat16)
                low = pl.ds(pl.multiple_of(size + turn * 16, 16), 16)
                back[member, low, :] = (-factor * imag).astype(jnp.bfloat16)
            return carry

        lax.fori_loop(0, size // 16, body, 0)

    @pl.when(step >= 4)
    def _():
        for half in range(2):
            held[step - 4, half] = dot(rows_ref[0, half], back[step - 4])

    @pl.when(step == 7)
    def _():
        for half in range(2):
            out_ref, place = (out_refs[0], 16 * half) if len(out_refs) == 1 else (out_refs[half], 0)
            pack_owners(lambda member, at, half=half: held[member, half, at, :], out_ref, place)


def middle(weights, got, counts, cols, rows, split):
    owners, _, lanes4 = got.shape
    size = rows.shape[2]
    lanes = lanes4 // 2
    if split:
        shapes = [(owners, 16, lanes)] * 2
    else:
        shapes = [(owners, 32, lanes)]
    return pl.pallas_call(
        middle_kernel,
        grid=(8,),
        in_specs=[
            pl.BlockSpec(memory_space=pltpu.SMEM),
            pl.BlockSpec(got.shape, lambda t: (0, 0, 0)),
            pl.BlockSpec(counts.shape, lambda t: (0, 0)),
            pl.BlockSpec((1, 2, size, 2 * size), lambda t: (jnp.minimum(t, 3), 0, 0, 0)),
            pl.BlockSpec((1, 2, size, 2 * size), lambda t: (jnp.maximum(t - 4, 0), 0, 0, 0)),
        ],
        out_specs=[pl.BlockSpec(shape, lambda t: (0, 0, 0)) for shape in shapes],
        out_shape=[jax.ShapeDtypeStruct(shape, jnp.bfloat16) for shape in shapes],
        scratch_shapes=[
            pltpu.VMEM((4, 2 * size, lanes), jnp.bfloat16),
            pltpu.VMEM((4, 2, size, lanes), jnp.float32),
            pltpu.VMEM((4, 2 * size, lanes), jnp.bfloat16),
            pltpu.VMEM((4, 2, size, lanes), jnp.float32),
        ],
        compiler_params=params(),
        cost_estimate=pl.CostEstimate(flops=9_000_000_000, bytes_accessed=22 << 20, transcendentals=0),
        name="middle",
    )(weights, got, counts, cols, rows)


def turn_rows(got_ref, wide, group, frames, members, first_row, first_lane):
    owners = got_ref.shape[0]
    piece = got_ref[:, first_row : first_row + 16, group * frames : (group + 1) * frames]
    turned = jnp.swapaxes(piece.astype(jnp.float32), 0, 1).astype(jnp.bfloat16)
    for member in range(members):
        for part in range(2):
            at = (2 * part + group) * owners
            for row in range(2):
                lane = first_lane + row * frames
                wide[member, at : at + owners, lane : lane + frames] = turned[4 * member + 2 * part + row]


def early_kernel(got_ref, cols_ref, out_ref, wide):
    member = pl.program_id(0)
    frames = got_ref.shape[2] // 2

    @pl.when(member == 0)
    def _():
        for half in range(2):
            for group in range(2):
                turn_rows(got_ref, wide, group, frames, 4, 16 * half, 2 * half * frames)

    for part in range(2):
        out_ref[0, part] = dot(cols_ref[0, part], wide[member]).astype(jnp.bfloat16)


def early_part(got, cols):
    owners, rows, lanes = got.shape
    size = cols.shape[2]
    return pl.pallas_call(
        early_kernel,
        grid=(4,),
        in_specs=[
            pl.BlockSpec(got.shape, lambda t: (0, 0, 0)),
            pl.BlockSpec((1, 2, size, size), lambda t: (t, 0, 0, 0)),
        ],
        out_specs=pl.BlockSpec((1, 2, size, 2 * lanes), lambda t: (t, 0, 0, 0)),
        out_shape=jax.ShapeDtypeStruct((4, 2, size, 2 * lanes), jnp.bfloat16),
        scratch_shapes=[pltpu.VMEM((4, size, 2 * lanes), jnp.bfloat16)],
        compiler_params=params(),
        cost_estimate=pl.CostEstimate(flops=4_000_000_000, bytes_accessed=10 << 20, transcendentals=0),
        name="early_part",
    )(got, cols)


def last_kernel(
    place_ref, scales_ref, late_ref, real_cols_ref, imag_cols_ref, real_part_ref, imag_part_ref, zb_ref,
    wave_ref, amp_ref, *rest,
):
    out_refs, (wide, field, sum_amp, sum_phase) = rest[:-4], rest[-4:]
    member = pl.program_id(0)
    frames = late_ref.shape[2] // 2
    cells_y, cells_z = amp_ref.shape[1:]

    @pl.when(member == 0)
    def _():
        for group in range(2):
            turn_rows(late_ref, wide, group, frames, 4, 0, 0)
        sum_amp[...] = jnp.zeros_like(sum_amp)
        sum_phase[...] = jnp.zeros_like(sum_phase)

    columns = wide[member]
    real = (dot(real_cols_ref[0, 0], columns) + real_part_ref[0, 0].astype(jnp.float32)).astype(jnp.bfloat16)
    imag = (dot(imag_cols_ref[0, 0], columns) + imag_part_ref[0, 0].astype(jnp.float32)).astype(jnp.bfloat16)
    for row in range(2):
        lane = slice(row * frames, (row + 1) * frames)
        field[row, :, 0:frames] = real[:, lane]
        field[row, :, frames : 2 * frames] = imag[:, lane]
    scale = scales_ref[member]
    tile = 256

    def body(step, carry):
        at = pl.ds(pl.multiple_of(step * tile, tile), tile)
        for row in range(2):
            both = dot(field[row, at, :], zb_ref[0])
            back_real, back_imag = both[:, 0:cells_z], both[:, cells_z : 2 * cells_z]
            wave_real = wave_ref[0, row, at, 0:cells_z].astype(jnp.float32)
            wave_imag = wave_ref[0, row, at, cells_z : 2 * cells_z].astype(jnp.float32)
            sum_amp[row, at, :] += back_real * wave_real - back_imag * wave_imag
            sum_phase[row, at, :] += scale * (back_real * wave_imag + back_imag * wave_real)
        return carry

    lax.fori_loop(0, cells_y // tile, body, 0)

    @pl.when(member == 3)
    def _():
        def close(step, carry):
            at = pl.ds(pl.multiple_of(step * tile, tile), tile)
            for row in range(2):
                out_ref, place = (out_refs[0], row) if len(out_refs) == 1 else (out_refs[row], 0)
                total = sum_amp[row, at, :] / amp_ref[row, at, :].astype(jnp.float32)
                out_ref[place, 0, at, :] = total.astype(jnp.bfloat16)
                out_ref[place, 1, at, :] = sum_phase[row, at, :].astype(jnp.bfloat16)
            return carry

        lax.fori_loop(0, cells_y // tile, close, 0)


def last(place, scales, late, early, cols, zb, wave, amp, half, pieces):
    _, cells_y, cells_z = amp.shape
    owners, _, lanes = late.shape
    size = cols.shape[2]

    def of_part(part, at):
        return lambda t, *_: (t, part, 0, at)

    return pl.pallas_call(
        last_kernel,
        grid_spec=pltpu.PrefetchScalarGridSpec(
            num_scalar_prefetch=2,
            grid=(4,),
            in_specs=[
                pl.BlockSpec((owners, 16, lanes), lambda t, *_: (0, 0, 0)),
                pl.BlockSpec((1, 1, size, size), of_part(0, 1)),
                pl.BlockSpec((1, 1, size, size), of_part(1, 1)),
                pl.BlockSpec((1, 1, size, lanes), of_part(0, half)),
                pl.BlockSpec((1, 1, size, lanes), of_part(1, half)),
                pl.BlockSpec((1,) + zb.shape[1:], lambda t, *_: (t, 0, 0)),
                pl.BlockSpec((1, 2, cells_y, 2 * cells_z), lambda t, *_: (t, half, 0, 0)),
                pl.BlockSpec((2, cells_y, cells_z), lambda t, p, *_: (2 * p[0] + half, 0, 0)),
            ],
            out_specs=[pl.BlockSpec((2 // pieces, 2, cells_y, cells_z), lambda t, *_: (0, 0, 0, 0))] * pieces,
            scratch_shapes=[
                pltpu.VMEM((4, size, lanes), jnp.bfloat16),
                pltpu.VMEM((2, cells_y, lanes), jnp.bfloat16),
                pltpu.VMEM((2, cells_y, cells_z), jnp.float32),
                pltpu.VMEM((2, cells_y, cells_z), jnp.float32),
            ],
        ),
        out_shape=[jax.ShapeDtypeStruct((2 // pieces, 2, cells_y, cells_z), jnp.bfloat16)] * pieces,
        compiler_params=params(),
        cost_estimate=pl.CostEstimate(flops=4_000_000_000, bytes_accessed=16 << 20, transcendentals=0),
        name="last",
    )(place, scales, late, cols, cols, early, early, zb, wave, amp)


def finish_kernel(place_ref, bragg_ref, sums_ref, amp_ref, disp_ref, *rest):
    new_amp_ref, new_disp_ref = rest[-2:]
    new_amp_ref[0] = amp_ref[0].astype(jnp.float32) - step_size * sums_ref[0, 0].astype(jnp.float32)
    sum_phase = sums_ref[0, 1].astype(jnp.float32)
    for axis in range(3):
        new_disp_ref[axis, 0] = (
            disp_ref[axis, 0].astype(jnp.float32) + (step_size * bragg_ref[axis]) * sum_phase
        ).astype(jnp.bfloat16)


def finish(place, bragg, sums, amp, disp, earlier, first_row, other):
    rows = sums.shape[0]
    _, cells_y, cells_z = amp.shape

    def row(t, p):
        half = 1 - p[0] if other else p[0]
        return 4 * half + first_row + t

    amp_spec = pl.BlockSpec((1, cells_y, cells_z), lambda t, p, *_: (row(t, p), 0, 0))
    disp_spec = pl.BlockSpec((3, 1, cells_y, cells_z), lambda t, p, *_: (0, row(t, p), 0, 0))
    kept = [] if earlier is None else list(earlier)
    return pl.pallas_call(
        finish_kernel,
        grid_spec=pltpu.PrefetchScalarGridSpec(
            num_scalar_prefetch=2,
            grid=(rows,),
            in_specs=[
                pl.BlockSpec((1, 2, cells_y, cells_z), lambda t, *_: (t, 0, 0, 0)),
                amp_spec,
                disp_spec,
            ]
            + [pl.BlockSpec(memory_space=pl.ANY)] * len(kept),
            out_specs=[amp_spec, disp_spec],
        ),
        out_shape=[
            jax.ShapeDtypeStruct(amp.shape, jnp.float32),
            jax.ShapeDtypeStruct(disp.shape, jnp.bfloat16),
        ],
        input_output_aliases={} if earlier is None else {5: 0, 6: 1},
        compiler_params=params(small_limit),
        cost_estimate=pl.CostEstimate(flops=10_000_000, bytes_accessed=(3 << 20) * rows, transcendentals=0),
        name="finish",
    )(place, bragg, sums, amp, disp, *kept)


def exchange(blocks):
    return lax.all_to_all(blocks, both_axes, split_axis=0, concat_axis=0, tiled=True)


def swap(values):
    return lax.ppermute(values, "spec", [(0, 1), (1, 0)])


def nothing(*refs):
    pass


def after(values, *others):
    anywhere = pl.BlockSpec(memory_space=pl.ANY)
    return pl.pallas_call(
        nothing,
        in_specs=[anywhere] * (1 + len(others)),
        out_specs=anywhere,
        out_shape=jax.ShapeDtypeStruct(values.shape, values.dtype),
        input_output_aliases={0: 0},
        compiler_params=params(),
        name="after",
    )(values, *others)


def per_device(amplitude, displacement, support, counts, bin_weights, bin_scales, bragg_vector):
    place = lax.axis_index("spec").reshape(1).astype(jnp.int32)
    size, rows_y, frames = counts.shape
    cells_z = amplitude.shape[2]
    volume = (place, bragg_vector, bin_scales, displacement, amplitude, support)
    section, blocks = first_half(*volume, size, frames)
    sent_early = exchange(blocks)
    rows = row_matrices(bin_scales, size)
    wave = waves(*volume)
    sent_late = exchange(after(second_half(section, rows), sent_early, wave))
    cols, zb = column_matrices(bin_scales, size, cells_z, frames)
    mine = lax.dynamic_slice_in_dim(counts, place[0] * (rows_y // 2), rows_y // 2, axis=1)
    mine = mine.reshape(size, rows_y // 2 * frames)
    early_counts, late_counts = mine[:, 0 : 2 * frames], mine[:, 2 * frames : 4 * frames]
    (early,) = middle(bin_weights, sent_early, early_counts, cols, rows, False)
    early = exchange(after(early, sent_late))
    parts = middle(bin_weights, sent_late, late_counts, cols, rows, True)
    early_sum = early_part(early, cols)
    late = [exchange(after(parts[0], early))]
    late.append(exchange(after(parts[1], early_sum, late[0])))
    sums = []
    for half in range(2):
        parts = last(
            place, bin_scales, late[half], early_sum, cols, zb, wave, amplitude, half, 1 + half
        )
        for number, part in enumerate(parts):
            sums.append((2 * half + number, part, swap(part)))
    outs = None
    for other in (False, True):
        for row, mine, theirs in sums:
            outs = finish(
                place, bragg_vector, theirs if other else mine, amplitude, displacement, outs, row, other
            )
    return tuple(outs)


def solution(mesh):
    in_specs = (
        P("slab", None, None),
        P(None, "slab", None, None),
        P("slab", None, None),
        P(None, "slab", None),
        P(),
        P(),
        P(),
    )
    out_specs = (P("slab", None, None), P(None, "slab", None, None))
    return jax.shard_map(
        per_device, mesh=mesh, in_specs=in_specs, out_specs=out_specs, check_vma=False
    )
```

```python
import functools
import math

import jax
import jax.numpy as jnp
from jax import lax
from jax.experimental import pallas as pl
from jax.experimental.pallas import tpu as pltpu
from jax.sharding import PartitionSpec as P

step_size = 0.5
both_axes = ("slab", "spec")
vmem_limit = 63 * 1024 * 1024
small_limit = 36 * 1024 * 1024
cos_terms = (
    0.9999992117703129, -19.738980419471183, 64.92865850463387,
    -85.27162830147759, 58.7905066287335, -21.071108461812614,
)
sin_terms = (
    6.283184916984337, -41.34158926418227, 81.59994386457431,
    -76.61447586037943, 41.342889429509576, -12.4712447471884,
)


half_cos_terms = (1.4142040219808052, -6.977637477680364,
    5.71518850637918, -1.728213959543254)
half_sin_terms = (4.442879570076877, -7.307816738835657,
    3.597774399705265, -0.7911994115558773)


def scaled_cos_sin(turns, magnitude):
    rest = turns - jnp.round(turns)
    square = rest * rest
    cosine = half_cos_terms[3] * square + half_cos_terms[2]
    sine = half_sin_terms[3] * square + half_sin_terms[2]
    for level in (1, 0):
        cosine = cosine * square + half_cos_terms[level]
        sine = sine * square + half_sin_terms[level]
    sine = sine * rest
    scaled = magnitude * sine
    return magnitude - scaled * sine, scaled * cosine


def cos_sin_turns(turns, cos_series=cos_terms, sin_series=sin_terms):
    rest = turns - jnp.round(turns)
    square = rest * rest
    cosine = jnp.full_like(square, cos_series[-1])
    sine = jnp.full_like(square, sin_series[-1])
    for level in range(len(cos_series) - 2, -1, -1):
        cosine = cosine * square + cos_series[level]
        sine = sine * square + sin_series[level]
    return cosine, sine * rest


def chirp_parts(out_index, in_index, count_out, count_in, bin_scale):
    product = (out_index - count_out // 2) * (in_index - count_in // 2)
    fraction = (product & (count_in - 1)).astype(jnp.float32) * (1.0 / count_in)
    excess = (bin_scale - 1.0) * (product.astype(jnp.float32) * (1.0 / count_in))
    cosine, sine = cos_sin_turns(fraction + excess)
    normalizer = 1.0 / math.sqrt(count_in)
    return cosine * normalizer, sine * -normalizer


def iota(shape, dim):
    return lax.broadcasted_iota(jnp.int32, shape, dim)


def dot(a, b):
    return jnp.dot(a, b, preferred_element_type=jnp.float32)


def params(limit=vmem_limit):
    return pltpu.CompilerParams(vmem_limit_bytes=limit)


def small_table(index, stride, others, size, bin_scale):
    product = stride * index * others
    fraction = (product & (size - 1)).astype(jnp.float32) * (1.0 / size)
    excess = (bin_scale - 1.0) * (product.astype(jnp.float32) * (1.0 / size))
    cosine, sine = cos_sin_turns(fraction + excess)
    return cosine, -sine


def fill_tables(big_real, big_imag, lane_index, size, bin_scale):
    others = lane_index - size // 2
    wide = (size // 8, size)
    real, imag = small_table(iota(wide, 0) - size // 16, 8, jnp.broadcast_to(others, wide), size, bin_scale)
    normalizer = 1.0 / math.sqrt(size)
    big_real[...] = real * normalizer
    big_imag[...] = imag * normalizer
    narrow = (8, size)
    return small_table(iota(narrow, 0), 1, jnp.broadcast_to(others, narrow), size, bin_scale)


def table_rows(big_real, big_imag, small, step):
    real = jnp.broadcast_to(big_real[pl.ds(step, 1), :], small[0].shape)
    imag = jnp.broadcast_to(big_imag[pl.ds(step, 1), :], small[0].shape)
    return real * small[0] - imag * small[1], real * small[1] + imag * small[0]


def fill_z(zf_ref, member, bin_scale, cells_z, frames):
    real, imag = chirp_parts(
        iota((cells_z, frames), 1), iota((cells_z, frames), 0), frames, cells_z, bin_scale
    )
    zf_ref[member, 0:cells_z, 0:frames] = real.astype(jnp.bfloat16)
    zf_ref[member, 0:cells_z, frames : 2 * frames] = imag.astype(jnp.bfloat16)
    zf_ref[member, cells_z : 2 * cells_z, 0:frames] = (-imag).astype(jnp.bfloat16)
    zf_ref[member, cells_z : 2 * cells_z, frames : 2 * frames] = real.astype(jnp.bfloat16)


def row_matrices_kernel(scales_ref, rows_ref, big_real, big_imag, *, size):
    bin_scale = scales_ref[pl.program_id(0)]
    small = fill_tables(big_real, big_imag, iota((1, size), 1), size, bin_scale)
    low = (iota((8, size), 0) & 2) == 0

    def body(step, carry):
        halves = [[[], []], [[], []]]
        for sub in range(2):
            real, imag = table_rows(big_real, big_imag, small, 2 * step + sub)
            for column, (first, second) in enumerate(((real, imag), (-imag, real))):
                halves[0][column].append(jnp.where(low, first, pltpu.roll(second, 2, 0)))
                halves[1][column].append(jnp.where(low, pltpu.roll(first, 6, 0), second))
        at = pl.ds(pl.multiple_of(16 * step, 16), 16)
        for half in range(2):
            for column in range(2):
                rows_ref[0, half, at, column * size : (column + 1) * size] = jnp.concatenate(
                    halves[half][column], axis=0
                ).astype(jnp.bfloat16)
        return carry

    lax.fori_loop(0, size // 16, body, 0)


def row_matrices(bin_scales, size):
    bins = bin_scales.shape[0]
    return pl.pallas_call(
        functools.partial(row_matrices_kernel, size=size),
        grid=(bins,),
        in_specs=[pl.BlockSpec(memory_space=pltpu.SMEM)],
        out_specs=pl.BlockSpec((1, 2, size, 2 * size), lambda b: (b, 0, 0, 0)),
        out_shape=jax.ShapeDtypeStruct((bins, 2, size, 2 * size), jnp.bfloat16),
        scratch_shapes=[pltpu.VMEM((size // 8, size), jnp.float32)] * 2,
        compiler_params=params(),
        cost_estimate=pl.CostEstimate(flops=4_000_000_000, bytes_accessed=8 << 20, transcendentals=0),
        name="row_matrices",
    )(bin_scales)


def column_matrices_kernel(scales_ref, cols_ref, zb_ref, big_real, big_imag, *, size, cells_z, frames):
    bin_scale = scales_ref[pl.program_id(0)]
    owners = size // 4
    lane = iota((1, size), 1)
    small = fill_tables(big_real, big_imag, 4 * (lane % owners) + lane // owners, size, bin_scale)
    wide = size // 2

    def body(step, carry):
        pairs = [table_rows(big_real, big_imag, small, 2 * step + sub) for sub in range(2)]
        real = jnp.concatenate([pair[0] for pair in pairs], axis=0)
        imag = jnp.concatenate([pair[1] for pair in pairs], axis=0)
        at = pl.ds(pl.multiple_of(16 * step, 16), 16)
        for part, (first, second) in enumerate(((real, -imag), (imag, real))):
            for half in range(2):
                lanes = slice(half * wide, (half + 1) * wide)
                cols_ref[0, part, at, 2 * half * wide : (2 * half + 1) * wide] = first[:, lanes].astype(jnp.bfloat16)
                cols_ref[0, part, at, (2 * half + 1) * wide : (2 * half + 2) * wide] = second[:, lanes].astype(jnp.bfloat16)
        return carry

    lax.fori_loop(0, size // 16, body, 0)
    real, imag = chirp_parts(
        iota((frames, cells_z), 0), iota((frames, cells_z), 1), frames, cells_z, bin_scale
    )
    zb_ref[0, 0:frames, 0:cells_z] = real.astype(jnp.bfloat16)
    zb_ref[0, 0:frames, cells_z : 2 * cells_z] = imag.astype(jnp.bfloat16)
    zb_ref[0, frames : 2 * frames, 0:cells_z] = (-imag).astype(jnp.bfloat16)
    zb_ref[0, frames : 2 * frames, cells_z : 2 * cells_z] = real.astype(jnp.bfloat16)


def column_matrices(bin_scales, size, cells_z, frames):
    bins = bin_scales.shape[0]
    return pl.pallas_call(
        functools.partial(column_matrices_kernel, size=size, cells_z=cells_z, frames=frames),
        grid=(bins,),
        in_specs=[pl.BlockSpec(memory_space=pltpu.SMEM)],
        out_specs=[
            pl.BlockSpec((1, 2, size, 2 * size), lambda b: (b, 0, 0, 0)),
            pl.BlockSpec((1, 2 * frames, 2 * cells_z), lambda b: (b, 0, 0)),
        ],
        out_shape=[
            jax.ShapeDtypeStruct((bins, 2, size, 2 * size), jnp.bfloat16),
            jax.ShapeDtypeStruct((bins, 2 * frames, 2 * cells_z), jnp.bfloat16),
        ],
        scratch_shapes=[pltpu.VMEM((size // 8, size), jnp.float32)] * 2,
        compiler_params=params(),
        cost_estimate=pl.CostEstimate(flops=4_000_000_000, bytes_accessed=8 << 20, transcendentals=0),
        name="column_matrices",
    )(bin_scales)


def pack_owners(values, out_ref, place):
    lanes = out_ref.shape[2]
    tile = 8

    def body(step, carry):
        at = pl.ds(pl.multiple_of(step * 4 * tile, 4 * tile), 4 * tile)
        rows = [values(member, at).reshape(tile // 2, 8, lanes) for member in range(4)]
        low = iota(rows[0].shape, 1) < 4
        even, odd = [], []
        for first, second in ((rows[0], rows[1]), (rows[2], rows[3])):
            even.append(jnp.where(low, first, pltpu.roll(second, 4, 1)))
            odd.append(jnp.where(low, pltpu.roll(first, 4, 1), second))
        even = jnp.concatenate(even, axis=1)
        odd = jnp.concatenate(odd, axis=1)
        both = jnp.stack([even, odd], axis=1).reshape(tile, 16, lanes)
        out_ref[pl.ds(step * tile, tile), pl.ds(place, 16), :] = both.astype(jnp.bfloat16)
        return carry

    lax.fori_loop(0, out_ref.shape[0] // tile, body, 0)


def wave_chunk(bragg_ref, scales_ref, disp_ref, amp_ref, mask_ref, row, at, use):
    phase = (
        bragg_ref[0] * disp_ref[0, row, at, :].astype(jnp.float32)
        + bragg_ref[1] * disp_ref[1, row, at, :].astype(jnp.float32)
        + bragg_ref[2] * disp_ref[2, row, at, :].astype(jnp.float32)
    )
    magnitude = amp_ref[row, at, :].astype(jnp.float32) * mask_ref[row, at, :].astype(jnp.float32)
    for member in range(4):
        real, imag = scaled_cos_sin((scales_ref[member] * (0.5 / math.pi)) * phase, magnitude)
        use(
            member,
            jnp.concatenate(
                [real.astype(jnp.bfloat16), imag.astype(jnp.bfloat16)], axis=1
            ),
        )


def wave_kernel(place_ref, bragg_ref, scales_ref, disp_ref, amp_ref, mask_ref, wave_ref):
    tile = 64

    def body(step, carry):
        at = pl.ds(pl.multiple_of(step * tile, tile), tile)

        def use(member, wave):
            wave_ref[member, 0, at, :] = wave

        wave_chunk(bragg_ref, scales_ref, disp_ref, amp_ref, mask_ref, 0, at, use)
        return carry

    lax.fori_loop(0, amp_ref.shape[1] // tile, body, 0)


def volume_specs(cells_y, cells_z, at_row):
    return [
        pl.BlockSpec((3, 1, cells_y, cells_z), lambda t, p, *_: (0, 4 * p[0] + at_row(t), 0, 0)),
        pl.BlockSpec((1, cells_y, cells_z), lambda t, p, *_: (4 * p[0] + at_row(t), 0, 0)),
        pl.BlockSpec((1, cells_y, cells_z), lambda t, p, *_: (4 * p[0] + at_row(t), 0, 0)),
    ]


def waves(place, bragg, scales, disp, amp, mask):
    _, _, cells_y, cells_z = disp.shape
    return pl.pallas_call(
        wave_kernel,
        grid_spec=pltpu.PrefetchScalarGridSpec(
            num_scalar_prefetch=3,
            grid=(4,),
            in_specs=volume_specs(cells_y, cells_z, lambda t: t),
            out_specs=pl.BlockSpec((4, 1, cells_y, 2 * cells_z), lambda t, *_: (0, t, 0, 0)),
        ),
        out_shape=jax.ShapeDtypeStruct((4, 4, cells_y, 2 * cells_z), jnp.bfloat16),
        compiler_params=params(),
        cost_estimate=pl.CostEstimate(flops=10_000_000_000, bytes_accessed=24 << 20, transcendentals=0),
        name="waves",
    )(place, bragg, scales, disp, amp, mask)


def first_kernel(
    place_ref, bragg_ref, scales_ref, disp_ref, amp_ref, mask_ref,
    section_ref, out_ref, section, held, zf, matrix, big_real, big_imag,
):
    step = pl.program_id(0)
    cells_y, cells_z = amp_ref.shape[1:]
    frames = zf.shape[2] // 2
    size = matrix.shape[0]

    @pl.when(step == 0)
    def _():
        for member in range(4):
            fill_z(zf, member, scales_ref[member], cells_z, frames)

    @pl.when(step < 4)
    def _():
        lanes = pl.ds(pl.multiple_of(step * frames, frames), frames)
        tile = cells_y // 2
        for turn in range(2):
            at = slice(turn * tile, (turn + 1) * tile)
            low = slice(cells_y + turn * tile, cells_y + (turn + 1) * tile)

            def use(member, wave, at=at, low=low):
                both = dot(wave, zf[member]).astype(jnp.bfloat16)
                section[member, at, lanes] = both[:, 0:frames]
                section[member, low, lanes] = both[:, frames : 2 * frames]

            wave_chunk(bragg_ref, scales_ref, disp_ref, amp_ref, mask_ref, 0, at, use)

    @pl.when(step >= 4)
    def _():
        small = fill_tables(big_real, big_imag, iota((1, size), 1), size, scales_ref[step - 4])
        low = (iota((8, size), 0) & 2) == 0

        section_ref[0] = section[step - 4]
        chunk = size // 2
        for piece in range(2):
            columns = [[], []]
            for turn in range(piece * chunk // 8, (piece + 1) * chunk // 8):
                real, imag = table_rows(big_real, big_imag, small, turn)
                columns[0].append(jnp.where(low, real, pltpu.roll(imag, 2, 0)))
                columns[1].append(jnp.where(low, -imag, pltpu.roll(real, 2, 0)))
            both = [jnp.concatenate(column, axis=0).astype(jnp.bfloat16) for column in columns]
            held[step - 4, piece * chunk : (piece + 1) * chunk, :] = dot(
                jnp.concatenate(both, axis=1), section[step - 4]
            )

    @pl.when(step == 7)
    def _():
        pack_owners(lambda member, at: held[member, at, :], out_ref, 0)


def first_half(place, bragg, scales, disp, amp, mask, size, frames):
    _, _, cells_y, cells_z = disp.shape
    owners = size // 4
    return pl.pallas_call(
        first_kernel,
        grid_spec=pltpu.PrefetchScalarGridSpec(
            num_scalar_prefetch=3,
            grid=(8,),
            in_specs=volume_specs(cells_y, cells_z, lambda t: jnp.minimum(t, 3)),
            out_specs=[
                pl.BlockSpec((1, 2 * cells_y, 4 * frames), lambda t, *_: (jnp.maximum(t - 4, 0), 0, 0)),
                pl.BlockSpec((owners, 16, 4 * frames), lambda t, *_: (0, 0, 0)),
            ],
            scratch_shapes=[
                pltpu.VMEM((4, 2 * cells_y, 4 * frames), jnp.bfloat16),
                pltpu.VMEM((4, size, 4 * frames), jnp.float32),
                pltpu.VMEM((4, 2 * cells_z, 2 * frames), jnp.bfloat16),
                pltpu.VMEM((size, 2 * size), jnp.bfloat16),
                pltpu.VMEM((size // 8, size), jnp.float32),
                pltpu.VMEM((size // 8, size), jnp.float32),
            ],
        ),
        out_shape=[
            jax.ShapeDtypeStruct((4, 2 * cells_y, 4 * frames), jnp.bfloat16),
            jax.ShapeDtypeStruct((owners, 16, 4 * frames), jnp.bfloat16),
        ],
        compiler_params=params(),
        cost_estimate=pl.CostEstimate(flops=9_000_000_000, bytes_accessed=14 << 20, transcendentals=0),
        name="first_half",
    )(place, bragg, scales, disp, amp, mask)


def second_kernel(section_ref, rows_ref, out_ref, held):
    step = pl.program_id(0)
    held[step] = dot(rows_ref[0, 0], section_ref[0])

    @pl.when(step == 3)
    def _():
        pack_owners(lambda member, at: held[member, at, :], out_ref, 0)


def second_half(section, rows):
    size = rows.shape[2]
    lanes = section.shape[2]
    owners = size // 4
    return pl.pallas_call(
        second_kernel,
        grid=(4,),
        in_specs=[
            pl.BlockSpec((1, 2 * size, lanes), lambda t: (t, 0, 0)),
            pl.BlockSpec((1, 1, size, 2 * size), lambda t: (t, 1, 0, 0)),
        ],
        out_specs=pl.BlockSpec((owners, 16, lanes), lambda t: (0, 0, 0)),
        out_shape=jax.ShapeDtypeStruct((owners, 16, lanes), jnp.bfloat16),
        scratch_shapes=[pltpu.VMEM((4, size, lanes), jnp.float32)],
        compiler_params=params(),
        cost_estimate=pl.CostEstimate(flops=3_000_000_000, bytes_accessed=10 << 20, transcendentals=0),
        name="second_half",
    )(section, rows)


def middle_kernel(weights_ref, got_ref, counts_ref, cols_ref, rows_ref, *rest):
    out_refs, (wide, far, back, held) = rest[:-4], rest[-4:]
    step = pl.program_id(0)
    owners = got_ref.shape[0]
    size = far.shape[2]
    frames = got_ref.shape[2] // 4
    lanes = 2 * frames

    @pl.when(step == 0)
    def _():
        for group in range(4):
            piece = got_ref[:, :, group * frames : (group + 1) * frames].astype(jnp.float32)
            turned = jnp.swapaxes(piece, 0, 1).astype(jnp.bfloat16)
            for member in range(4):
                for part in range(2):
                    at = (4 * (group // 2) + 2 * part + group % 2) * owners
                    for row in range(2):
                        wide[member, at : at + owners, row * frames : (row + 1) * frames] = turned[
                            4 * member + 2 * part + row
                        ]

    @pl.when(step < 4)
    def _():
        for part in range(2):
            far[step, part] = dot(cols_ref[0, part], wide[step])

    @pl.when(step == 3)
    def _():
        def body(turn, carry):
            at = pl.ds(pl.multiple_of(turn * 16, 16), 16)
            fields = [(far[member, 0, at, :], far[member, 1, at, :]) for member in range(4)]
            intensity = None
            for member, (real, imag) in enumerate(fields):
                term = weights_ref[member] * (real * real + imag * imag)
                intensity = term if intensity is None else intensity + term
            ratio = 1.0 - jnp.sqrt(counts_ref[at, :].astype(jnp.float32) / jnp.maximum(intensity, 0.5))
            for member, (real, imag) in enumerate(fields):
                factor = weights_ref[member] * ratio
                back[member, at, :] = (factor * real).astype(jnp.bfloat16)
                low = pl.ds(pl.multiple_of(size + turn * 16, 16), 16)
                back[member, low, :] = (-factor * imag).astype(jnp.bfloat16)
            return carry

        lax.fori_loop(0, size // 16, body, 0)

    @pl.when(step >= 4)
    def _():
        for half in range(2):
            held[step - 4, half] = dot(rows_ref[0, half], back[step - 4])

    @pl.when(step == 7)
    def _():
        for half in range(2):
            out_ref, place = (out_refs[0], 16 * half) if len(out_refs) == 1 else (out_refs[half], 0)
            pack_owners(lambda member, at, half=half: held[member, half, at, :], out_ref, place)


def middle(weights, got, counts, cols, rows, split):
    owners, _, lanes4 = got.shape
    size = rows.shape[2]
    lanes = lanes4 // 2
    if split:
        shapes = [(owners, 16, lanes)] * 2
    else:
        shapes = [(owners, 32, lanes)]
    return pl.pallas_call(
        middle_kernel,
        grid=(8,),
        in_specs=[
            pl.BlockSpec(memory_space=pltpu.SMEM),
            pl.BlockSpec(got.shape, lambda t: (0, 0, 0)),
            pl.BlockSpec(counts.shape, lambda t: (0, 0)),
            pl.BlockSpec((1, 2, size, 2 * size), lambda t: (jnp.minimum(t, 3), 0, 0, 0)),
            pl.BlockSpec((1, 2, size, 2 * size), lambda t: (jnp.maximum(t - 4, 0), 0, 0, 0)),
        ],
        out_specs=[pl.BlockSpec(shape, lambda t: (0, 0, 0)) for shape in shapes],
        out_shape=[jax.ShapeDtypeStruct(shape, jnp.bfloat16) for shape in shapes],
        scratch_shapes=[
            pltpu.VMEM((4, 2 * size, lanes), jnp.bfloat16),
            pltpu.VMEM((4, 2, size, lanes), jnp.float32),
            pltpu.VMEM((4, 2 * size, lanes), jnp.bfloat16),
            pltpu.VMEM((4, 2, size, lanes), jnp.float32),
        ],
        compiler_params=params(),
        cost_estimate=pl.CostEstimate(flops=9_000_000_000, bytes_accessed=22 << 20, transcendentals=0),
        name="middle",
    )(weights, got, counts, cols, rows)


def turn_rows(got_ref, wide, group, frames, members, first_row, first_lane):
    owners = got_ref.shape[0]
    piece = got_ref[:, first_row : first_row + 16, group * frames : (group + 1) * frames]
    turned = jnp.swapaxes(piece.astype(jnp.float32), 0, 1).astype(jnp.bfloat16)
    for member in range(members):
        for part in range(2):
            at = (2 * part + group) * owners
            for row in range(2):
                lane = first_lane + row * frames
                wide[member, at : at + owners, lane : lane + frames] = turned[4 * member + 2 * part + row]


def early_kernel(got_ref, cols_ref, out_ref, wide):
    member = pl.program_id(0)
    frames = got_ref.shape[2] // 2

    @pl.when(member == 0)
    def _():
        for half in range(2):
            for group in range(2):
                turn_rows(got_ref, wide, group, frames, 4, 16 * half, 2 * half * frames)

    for part in range(2):
        out_ref[0, part] = dot(cols_ref[0, part], wide[member]).astype(jnp.bfloat16)


def early_part(got, cols):
    owners, rows, lanes = got.shape
    size = cols.shape[2]
    return pl.pallas_call(
        early_kernel,
        grid=(4,),
        in_specs=[
            pl.BlockSpec(got.shape, lambda t: (0, 0, 0)),
            pl.BlockSpec((1, 2, size, size), lambda t: (t, 0, 0, 0)),
        ],
        out_specs=pl.BlockSpec((1, 2, size, 2 * lanes), lambda t: (t, 0, 0, 0)),
        out_shape=jax.ShapeDtypeStruct((4, 2, size, 2 * lanes), jnp.bfloat16),
        scratch_shapes=[pltpu.VMEM((4, size, 2 * lanes), jnp.bfloat16)],
        compiler_params=params(),
        cost_estimate=pl.CostEstimate(flops=4_000_000_000, bytes_accessed=10 << 20, transcendentals=0),
        name="early_part",
    )(got, cols)


def last_kernel(
    place_ref, scales_ref, late_ref, real_cols_ref, imag_cols_ref, real_part_ref, imag_part_ref, zb_ref,
    wave_ref, amp_ref, *rest,
):
    out_refs, (wide, field, sum_amp, sum_phase) = rest[:-4], rest[-4:]
    member = pl.program_id(0)
    frames = late_ref.shape[2] // 2
    cells_y, cells_z = amp_ref.shape[1:]

    @pl.when(member == 0)
    def _():
        for group in range(2):
            turn_rows(late_ref, wide, group, frames, 4, 0, 0)
        sum_amp[...] = jnp.zeros_like(sum_amp)
        sum_phase[...] = jnp.zeros_like(sum_phase)

    columns = wide[member]
    real = (dot(real_cols_ref[0, 0], columns) + real_part_ref[0, 0].astype(jnp.float32)).astype(jnp.bfloat16)
    imag = (dot(imag_cols_ref[0, 0], columns) + imag_part_ref[0, 0].astype(jnp.float32)).astype(jnp.bfloat16)
    for row in range(2):
        lane = slice(row * frames, (row + 1) * frames)
        field[row, :, 0:frames] = real[:, lane]
        field[row, :, frames : 2 * frames] = imag[:, lane]
    scale = scales_ref[member]
    tile = 256

    def body(step, carry):
        at = pl.ds(pl.multiple_of(step * tile, tile), tile)
        for row in range(2):
            both = dot(field[row, at, :], zb_ref[0])
            back_real, back_imag = both[:, 0:cells_z], both[:, cells_z : 2 * cells_z]
            wave_real = wave_ref[0, row, at, 0:cells_z].astype(jnp.float32)
            wave_imag = wave_ref[0, row, at, cells_z : 2 * cells_z].astype(jnp.float32)
            sum_amp[row, at, :] += back_real * wave_real - back_imag * wave_imag
            sum_phase[row, at, :] += scale * (back_real * wave_imag + back_imag * wave_real)
        return carry

    lax.fori_loop(0, cells_y // tile, body, 0)

    @pl.when(member == 3)
    def _():
        def close(step, carry):
            at = pl.ds(pl.multiple_of(step * tile, tile), tile)
            for row in range(2):
                out_ref, place = (out_refs[0], row) if len(out_refs) == 1 else (out_refs[row], 0)
                total = sum_amp[row, at, :] / amp_ref[row, at, :].astype(jnp.float32)
                out_ref[place, 0, at, :] = total.astype(jnp.bfloat16)
                out_ref[place, 1, at, :] = sum_phase[row, at, :].astype(jnp.bfloat16)
            return carry

        lax.fori_loop(0, cells_y // tile, close, 0)


def last(place, scales, late, early, cols, zb, wave, amp, half, pieces):
    _, cells_y, cells_z = amp.shape
    owners, _, lanes = late.shape
    size = cols.shape[2]

    def of_part(part, at):
        return lambda t, *_: (t, part, 0, at)

    return pl.pallas_call(
        last_kernel,
        grid_spec=pltpu.PrefetchScalarGridSpec(
            num_scalar_prefetch=2,
            grid=(4,),
            in_specs=[
                pl.BlockSpec((owners, 16, lanes), lambda t, *_: (0, 0, 0)),
                pl.BlockSpec((1, 1, size, size), of_part(0, 1)),
                pl.BlockSpec((1, 1, size, size), of_part(1, 1)),
                pl.BlockSpec((1, 1, size, lanes), of_part(0, half)),
                pl.BlockSpec((1, 1, size, lanes), of_part(1, half)),
                pl.BlockSpec((1,) + zb.shape[1:], lambda t, *_: (t, 0, 0)),
                pl.BlockSpec((1, 2, cells_y, 2 * cells_z), lambda t, *_: (t, half, 0, 0)),
                pl.BlockSpec((2, cells_y, cells_z), lambda t, p, *_: (2 * p[0] + half, 0, 0)),
            ],
            out_specs=[pl.BlockSpec((2 // pieces, 2, cells_y, cells_z), lambda t, *_: (0, 0, 0, 0))] * pieces,
            scratch_shapes=[
                pltpu.VMEM((4, size, lanes), jnp.bfloat16),
                pltpu.VMEM((2, cells_y, lanes), jnp.bfloat16),
                pltpu.VMEM((2, cells_y, cells_z), jnp.float32),
                pltpu.VMEM((2, cells_y, cells_z), jnp.float32),
            ],
        ),
        out_shape=[jax.ShapeDtypeStruct((2 // pieces, 2, cells_y, cells_z), jnp.bfloat16)] * pieces,
        compiler_params=params(),
        cost_estimate=pl.CostEstimate(flops=4_000_000_000, bytes_accessed=16 << 20, transcendentals=0),
        name="last",
    )(place, scales, late, cols, cols, early, early, zb, wave, amp)


def finish_kernel(place_ref, bragg_ref, sums_ref, amp_ref, disp_ref, *rest):
    new_amp_ref, new_disp_ref = rest[-2:]
    new_amp_ref[0] = amp_ref[0].astype(jnp.float32) - step_size * sums_ref[0, 0].astype(jnp.float32)
    sum_phase = sums_ref[0, 1].astype(jnp.float32)
    for axis in range(3):
        new_disp_ref[axis, 0] = (
            disp_ref[axis, 0].astype(jnp.float32) + (step_size * bragg_ref[axis]) * sum_phase
        ).astype(jnp.bfloat16)


def finish(place, bragg, sums, amp, disp, earlier, first_row, other):
    rows = sums.shape[0]
    _, cells_y, cells_z = amp.shape

    def row(t, p):
        half = 1 - p[0] if other else p[0]
        return 4 * half + first_row + t

    amp_spec = pl.BlockSpec((1, cells_y, cells_z), lambda t, p, *_: (row(t, p), 0, 0))
    disp_spec = pl.BlockSpec((3, 1, cells_y, cells_z), lambda t, p, *_: (0, row(t, p), 0, 0))
    kept = [] if earlier is None else list(earlier)
    return pl.pallas_call(
        finish_kernel,
        grid_spec=pltpu.PrefetchScalarGridSpec(
            num_scalar_prefetch=2,
            grid=(rows,),
            in_specs=[
                pl.BlockSpec((1, 2, cells_y, cells_z), lambda t, *_: (t, 0, 0, 0)),
                amp_spec,
                disp_spec,
            ]
            + [pl.BlockSpec(memory_space=pl.ANY)] * len(kept),
            out_specs=[amp_spec, disp_spec],
        ),
        out_shape=[
            jax.ShapeDtypeStruct(amp.shape, jnp.float32),
            jax.ShapeDtypeStruct(disp.shape, jnp.bfloat16),
        ],
        input_output_aliases={} if earlier is None else {5: 0, 6: 1},
        compiler_params=params(small_limit),
        cost_estimate=pl.CostEstimate(flops=10_000_000, bytes_accessed=(3 << 20) * rows, transcendentals=0),
        name="finish",
    )(place, bragg, sums, amp, disp, *kept)


def exchange(blocks):
    return lax.all_to_all(blocks, both_axes, split_axis=0, concat_axis=0, tiled=True)


def swap(values):
    return lax.ppermute(values, "spec", [(0, 1), (1, 0)])


def nothing(*refs):
    pass


def after(values, *others):
    anywhere = pl.BlockSpec(memory_space=pl.ANY)
    return pl.pallas_call(
        nothing,
        in_specs=[anywhere] * (1 + len(others)),
        out_specs=anywhere,
        out_shape=jax.ShapeDtypeStruct(values.shape, values.dtype),
        input_output_aliases={0: 0},
        compiler_params=params(),
        name="after",
    )(values, *others)


def per_device(amplitude, displacement, support, counts, bin_weights, bin_scales, bragg_vector):
    place = lax.axis_index("spec").reshape(1).astype(jnp.int32)
    size, rows_y, frames = counts.shape
    cells_z = amplitude.shape[2]
    volume = (place, bragg_vector, bin_scales, displacement, amplitude, support)
    section, blocks = first_half(*volume, size, frames)
    sent_early = exchange(blocks)
    rows = row_matrices(bin_scales, size)
    wave = waves(*volume)
    sent_late = exchange(after(second_half(section, rows), sent_early, wave))
    cols, zb = column_matrices(bin_scales, size, cells_z, frames)
    mine = lax.dynamic_slice_in_dim(counts, place[0] * (rows_y // 2), rows_y // 2, axis=1)
    mine = mine.reshape(size, rows_y // 2 * frames)
    early_counts, late_counts = mine[:, 0 : 2 * frames], mine[:, 2 * frames : 4 * frames]
    (early,) = middle(bin_weights, sent_early, early_counts, cols, rows, False)
    early = exchange(after(early, sent_late))
    parts = middle(bin_weights, sent_late, late_counts, cols, rows, True)
    early_sum = early_part(early, cols)
    late = [exchange(after(parts[0], early))]
    late.append(exchange(after(parts[1], early_sum, late[0])))
    sums = []
    for half in range(2):
        parts = last(
            place, bin_scales, late[half], early_sum, cols, zb, wave, amplitude, half, 1 + half
        )
        for number, part in enumerate(parts):
            sums.append((2 * half + number, part, swap(part)))
    outs = None
    for other in (False, True):
        for row, mine, theirs in sums:
            outs = finish(
                place, bragg_vector, theirs if other else mine, amplitude, displacement, outs, row, other
            )
    return tuple(outs)


def solution(mesh):
    in_specs = (
        P("slab", None, None),
        P(None, "slab", None, None),
        P("slab", None, None),
        P(None, "slab", None),
        P(),
        P(),
        P(),
    )
    out_specs = (P("slab", None, None), P(None, "slab", None, None))
    return jax.shard_map(
        per_device, mesh=mesh, in_specs=in_specs, out_specs=out_specs, check_vma=False
    )
```

```python
import functools
import math

import jax
import jax.numpy as jnp
from jax import lax
from jax.experimental import pallas as pl
from jax.experimental.pallas import tpu as pltpu
from jax.sharding import PartitionSpec as P

step_size = 0.5
both_axes = ("slab", "spec")
vmem_limit = 63 * 1024 * 1024
small_limit = 36 * 1024 * 1024
cos_terms = (
    0.9999992117703129, -19.738980419471183, 64.92865850463387,
    -85.27162830147759, 58.7905066287335, -21.071108461812614,
)
sin_terms = (
    6.283184916984337, -41.34158926418227, 81.59994386457431,
    -76.61447586037943, 41.342889429509576, -12.4712447471884,
)


half_cos_terms = (1.4142040219808052, -6.977637477680364,
    5.71518850637918, -1.728213959543254)
half_sin_terms = (4.442879570076877, -7.307816738835657,
    3.597774399705265, -0.7911994115558773)


def scaled_cos_sin(turns, magnitude):
    rest = turns - jnp.round(turns)
    square = rest * rest
    cosine = half_cos_terms[3] * square + half_cos_terms[2]
    sine = half_sin_terms[3] * square + half_sin_terms[2]
    for level in (1, 0):
        cosine = cosine * square + half_cos_terms[level]
        sine = sine * square + half_sin_terms[level]
    sine = sine * rest
    scaled = magnitude * sine
    return magnitude - scaled * sine, scaled * cosine


def cos_sin_turns(turns, cos_series=cos_terms, sin_series=sin_terms):
    rest = turns - jnp.round(turns)
    square = rest * rest
    cosine = jnp.full_like(square, cos_series[-1])
    sine = jnp.full_like(square, sin_series[-1])
    for level in range(len(cos_series) - 2, -1, -1):
        cosine = cosine * square + cos_series[level]
        sine = sine * square + sin_series[level]
    return cosine, sine * rest


def chirp_parts(out_index, in_index, count_out, count_in, bin_scale):
    product = (out_index - count_out // 2) * (in_index - count_in // 2)
    fraction = (product & (count_in - 1)).astype(jnp.float32) * (1.0 / count_in)
    excess = (bin_scale - 1.0) * (product.astype(jnp.float32) * (1.0 / count_in))
    cosine, sine = cos_sin_turns(fraction + excess)
    normalizer = 1.0 / math.sqrt(count_in)
    return cosine * normalizer, sine * -normalizer


def iota(shape, dim):
    return lax.broadcasted_iota(jnp.int32, shape, dim)


def dot(a, b):
    return jnp.dot(a, b, preferred_element_type=jnp.float32)


def params(limit=vmem_limit):
    return pltpu.CompilerParams(vmem_limit_bytes=limit)


def small_table(index, stride, others, size, bin_scale):
    product = stride * index * others
    fraction = (product & (size - 1)).astype(jnp.float32) * (1.0 / size)
    excess = (bin_scale - 1.0) * (product.astype(jnp.float32) * (1.0 / size))
    cosine, sine = cos_sin_turns(fraction + excess)
    return cosine, -sine


def fill_tables(big_real, big_imag, lane_index, size, bin_scale):
    others = lane_index - size // 2
    wide = (size // 8, size)
    real, imag = small_table(iota(wide, 0) - size // 16, 8, jnp.broadcast_to(others, wide), size, bin_scale)
    normalizer = 1.0 / math.sqrt(size)
    big_real[...] = real * normalizer
    big_imag[...] = imag * normalizer
    narrow = (8, size)
    return small_table(iota(narrow, 0), 1, jnp.broadcast_to(others, narrow), size, bin_scale)


def table_rows(big_real, big_imag, small, step):
    real = jnp.broadcast_to(big_real[pl.ds(step, 1), :], small[0].shape)
    imag = jnp.broadcast_to(big_imag[pl.ds(step, 1), :], small[0].shape)
    return real * small[0] - imag * small[1], real * small[1] + imag * small[0]


def fill_z(zf_ref, member, bin_scale, cells_z, frames):
    others = iota((1, frames), 1) - frames // 2
    wide, narrow = (cells_z // 8, frames), (8, frames)
    big_real, big_imag = small_table(
        iota(wide, 0) - cells_z // 16, 8, jnp.broadcast_to(others, wide), cells_z, bin_scale
    )
    low_real, low_imag = small_table(iota(narrow, 0), 1, jnp.broadcast_to(others, narrow), cells_z, bin_scale)
    normalizer = 1.0 / math.sqrt(cells_z)
    big_real, big_imag = (big_real * normalizer)[:, None, :], (big_imag * normalizer)[:, None, :]
    real = (big_real * low_real[None] - big_imag * low_imag[None]).reshape(cells_z, frames)
    imag = (big_real * low_imag[None] + big_imag * low_real[None]).reshape(cells_z, frames)
    zf_ref[member, 0:cells_z, 0:frames] = real.astype(jnp.bfloat16)
    zf_ref[member, 0:cells_z, frames : 2 * frames] = imag.astype(jnp.bfloat16)
    zf_ref[member, cells_z : 2 * cells_z, 0:frames] = (-imag).astype(jnp.bfloat16)
    zf_ref[member, cells_z : 2 * cells_z, frames : 2 * frames] = real.astype(jnp.bfloat16)


def row_matrices_kernel(scales_ref, rows_ref, big_real, big_imag, *, size):
    bin_scale = scales_ref[pl.program_id(0)]
    small = fill_tables(big_real, big_imag, iota((1, size), 1), size, bin_scale)
    low = (iota((8, size), 0) & 2) == 0

    def body(step, carry):
        halves = [[[], []], [[], []]]
        for sub in range(2):
            real, imag = table_rows(big_real, big_imag, small, 2 * step + sub)
            for column, (first, second) in enumerate(((real, imag), (-imag, real))):
                halves[0][column].append(jnp.where(low, first, pltpu.roll(second, 2, 0)))
                halves[1][column].append(jnp.where(low, pltpu.roll(first, 6, 0), second))
        at = pl.ds(pl.multiple_of(16 * step, 16), 16)
        for half in range(2):
            for column in range(2):
                rows_ref[0, half, at, column * size : (column + 1) * size] = jnp.concatenate(
                    halves[half][column], axis=0
                ).astype(jnp.bfloat16)
        return carry

    lax.fori_loop(0, size // 16, body, 0)


def row_matrices(bin_scales, size):
    bins = bin_scales.shape[0]
    return pl.pallas_call(
        functools.partial(row_matrices_kernel, size=size),
        grid=(bins,),
        in_specs=[pl.BlockSpec(memory_space=pltpu.SMEM)],
        out_specs=pl.BlockSpec((1, 2, size, 2 * size), lambda b: (b, 0, 0, 0)),
        out_shape=jax.ShapeDtypeStruct((bins, 2, size, 2 * size), jnp.bfloat16),
        scratch_shapes=[pltpu.VMEM((size // 8, size), jnp.float32)] * 2,
        compiler_params=params(),
        cost_estimate=pl.CostEstimate(flops=4_000_000_000, bytes_accessed=8 << 20, transcendentals=0),
        name="row_matrices",
    )(bin_scales)


def column_matrices_kernel(scales_ref, cols_ref, zb_ref, big_real, big_imag, *, size, cells_z, frames):
    bin_scale = scales_ref[pl.program_id(0)]
    owners = size // 4
    lane = iota((1, size), 1)
    small = fill_tables(big_real, big_imag, 4 * (lane % owners) + lane // owners, size, bin_scale)
    wide = size // 2

    def body(step, carry):
        pairs = [table_rows(big_real, big_imag, small, 2 * step + sub) for sub in range(2)]
        real = jnp.concatenate([pair[0] for pair in pairs], axis=0)
        imag = jnp.concatenate([pair[1] for pair in pairs], axis=0)
        at = pl.ds(pl.multiple_of(16 * step, 16), 16)
        for part, (first, second) in enumerate(((real, -imag), (imag, real))):
            for half in range(2):
                lanes = slice(half * wide, (half + 1) * wide)
                cols_ref[0, part, at, 2 * half * wide : (2 * half + 1) * wide] = first[:, lanes].astype(jnp.bfloat16)
                cols_ref[0, part, at, (2 * half + 1) * wide : (2 * half + 2) * wide] = second[:, lanes].astype(jnp.bfloat16)
        return carry

    lax.fori_loop(0, size // 16, body, 0)
    real, imag = chirp_parts(
        iota((frames, cells_z), 0), iota((frames, cells_z), 1), frames, cells_z, bin_scale
    )
    zb_ref[0, 0:frames, 0:cells_z] = real.astype(jnp.bfloat16)
    zb_ref[0, 0:frames, cells_z : 2 * cells_z] = imag.astype(jnp.bfloat16)
    zb_ref[0, frames : 2 * frames, 0:cells_z] = (-imag).astype(jnp.bfloat16)
    zb_ref[0, frames : 2 * frames, cells_z : 2 * cells_z] = real.astype(jnp.bfloat16)


def column_matrices(bin_scales, size, cells_z, frames):
    bins = bin_scales.shape[0]
    return pl.pallas_call(
        functools.partial(column_matrices_kernel, size=size, cells_z=cells_z, frames=frames),
        grid=(bins,),
        in_specs=[pl.BlockSpec(memory_space=pltpu.SMEM)],
        out_specs=[
            pl.BlockSpec((1, 2, size, 2 * size), lambda b: (b, 0, 0, 0)),
            pl.BlockSpec((1, 2 * frames, 2 * cells_z), lambda b: (b, 0, 0)),
        ],
        out_shape=[
            jax.ShapeDtypeStruct((bins, 2, size, 2 * size), jnp.bfloat16),
            jax.ShapeDtypeStruct((bins, 2 * frames, 2 * cells_z), jnp.bfloat16),
        ],
        scratch_shapes=[pltpu.VMEM((size // 8, size), jnp.float32)] * 2,
        compiler_params=params(),
        cost_estimate=pl.CostEstimate(flops=4_000_000_000, bytes_accessed=8 << 20, transcendentals=0),
        name="column_matrices",
    )(bin_scales)


def pack_owners(values, out_ref, place):
    lanes = out_ref.shape[2]
    tile = 8

    def body(step, carry):
        at = pl.ds(pl.multiple_of(step * 4 * tile, 4 * tile), 4 * tile)
        rows = [values(member, at).reshape(tile // 2, 8, lanes) for member in range(4)]
        low = iota(rows[0].shape, 1) < 4
        even, odd = [], []
        for first, second in ((rows[0], rows[1]), (rows[2], rows[3])):
            even.append(jnp.where(low, first, pltpu.roll(second, 4, 1)))
            odd.append(jnp.where(low, pltpu.roll(first, 4, 1), second))
        even = jnp.concatenate(even, axis=1)
        odd = jnp.concatenate(odd, axis=1)
        both = jnp.stack([even, odd], axis=1).reshape(tile, 16, lanes)
        out_ref[pl.ds(step * tile, tile), pl.ds(place, 16), :] = both.astype(jnp.bfloat16)
        return carry

    lax.fori_loop(0, out_ref.shape[0] // tile, body, 0)


def wave_chunk(bragg_ref, scales_ref, disp_ref, amp_ref, mask_ref, row, at, use):
    phase = (
        bragg_ref[0] * disp_ref[0, row, at, :].astype(jnp.float32)
        + bragg_ref[1] * disp_ref[1, row, at, :].astype(jnp.float32)
        + bragg_ref[2] * disp_ref[2, row, at, :].astype(jnp.float32)
    )
    magnitude = amp_ref[row, at, :].astype(jnp.float32) * mask_ref[row, at, :].astype(jnp.float32)
    for member in range(4):
        real, imag = scaled_cos_sin((scales_ref[member] * (0.5 / math.pi)) * phase, magnitude)
        use(
            member,
            jnp.concatenate(
                [real.astype(jnp.bfloat16), imag.astype(jnp.bfloat16)], axis=1
            ),
        )


def wave_kernel(place_ref, bragg_ref, scales_ref, disp_ref, amp_ref, mask_ref, wave_ref):
    tile = 64

    def body(step, carry):
        at = pl.ds(pl.multiple_of(step * tile, tile), tile)

        def use(member, wave):
            wave_ref[member, 0, at, :] = wave

        wave_chunk(bragg_ref, scales_ref, disp_ref, amp_ref, mask_ref, 0, at, use)
        return carry

    lax.fori_loop(0, amp_ref.shape[1] // tile, body, 0)


def volume_specs(cells_y, cells_z, at_row):
    return [
        pl.BlockSpec((3, 1, cells_y, cells_z), lambda t, p, *_: (0, 4 * p[0] + at_row(t), 0, 0)),
        pl.BlockSpec((1, cells_y, cells_z), lambda t, p, *_: (4 * p[0] + at_row(t), 0, 0)),
        pl.BlockSpec((1, cells_y, cells_z), lambda t, p, *_: (4 * p[0] + at_row(t), 0, 0)),
    ]


def waves(place, bragg, scales, disp, amp, mask):
    _, _, cells_y, cells_z = disp.shape
    return pl.pallas_call(
        wave_kernel,
        grid_spec=pltpu.PrefetchScalarGridSpec(
            num_scalar_prefetch=3,
            grid=(4,),
            in_specs=volume_specs(cells_y, cells_z, lambda t: t),
            out_specs=pl.BlockSpec((4, 1, cells_y, 2 * cells_z), lambda t, *_: (0, t, 0, 0)),
        ),
        out_shape=jax.ShapeDtypeStruct((4, 4, cells_y, 2 * cells_z), jnp.bfloat16),
        compiler_params=params(),
        cost_estimate=pl.CostEstimate(flops=10_000_000_000, bytes_accessed=24 << 20, transcendentals=0),
        name="waves",
    )(place, bragg, scales, disp, amp, mask)


def first_kernel(
    place_ref, bragg_ref, scales_ref, disp_ref, amp_ref, mask_ref,
    section_ref, out_ref, section, held, zf, matrix, big_real, big_imag,
):
    step = pl.program_id(0)
    cells_y, cells_z = amp_ref.shape[1:]
    frames = zf.shape[2] // 2
    size = matrix.shape[0]

    @pl.when(step == 0)
    def _():
        for member in range(4):
            fill_z(zf, member, scales_ref[member], cells_z, frames)

    @pl.when(step < 4)
    def _():
        lanes = pl.ds(pl.multiple_of(step * frames, frames), frames)
        tile = cells_y // 2
        for turn in range(2):
            at = slice(turn * tile, (turn + 1) * tile)
            low = slice(cells_y + turn * tile, cells_y + (turn + 1) * tile)

            def use(member, wave, at=at, low=low):
                both = dot(wave, zf[member]).astype(jnp.bfloat16)
                section[member, at, lanes] = both[:, 0:frames]
                section[member, low, lanes] = both[:, frames : 2 * frames]

            wave_chunk(bragg_ref, scales_ref, disp_ref, amp_ref, mask_ref, 0, at, use)

    @pl.when(step >= 4)
    def _():
        small = fill_tables(big_real, big_imag, iota((1, size), 1), size, scales_ref[step - 4])
        low = (iota((8, size), 0) & 2) == 0

        section_ref[0] = section[step - 4]
        chunk = size // 2
        for piece in range(2):
            columns = [[], []]
            for turn in range(piece * chunk // 8, (piece + 1) * chunk // 8):
                real, imag = table_rows(big_real, big_imag, small, turn)
                columns[0].append(jnp.where(low, real, pltpu.roll(imag, 2, 0)))
                columns[1].append(jnp.where(low, -imag, pltpu.roll(real, 2, 0)))
            both = [jnp.concatenate(column, axis=0).astype(jnp.bfloat16) for column in columns]
            held[step - 4, piece * chunk : (piece + 1) * chunk, :] = dot(
                jnp.concatenate(both, axis=1), section[step - 4]
            )

    @pl.when(step == 7)
    def _():
        pack_owners(lambda member, at: held[member, at, :], out_ref, 0)


def first_half(place, bragg, scales, disp, amp, mask, size, frames):
    _, _, cells_y, cells_z = disp.shape
    owners = size // 4
    return pl.pallas_call(
        first_kernel,
        grid_spec=pltpu.PrefetchScalarGridSpec(
            num_scalar_prefetch=3,
            grid=(8,),
            in_specs=volume_specs(cells_y, cells_z, lambda t: jnp.minimum(t, 3)),
            out_specs=[
                pl.BlockSpec((1, 2 * cells_y, 4 * frames), lambda t, *_: (jnp.maximum(t - 4, 0), 0, 0)),
                pl.BlockSpec((owners, 16, 4 * frames), lambda t, *_: (0, 0, 0)),
            ],
            scratch_shapes=[
                pltpu.VMEM((4, 2 * cells_y, 4 * frames), jnp.bfloat16),
                pltpu.VMEM((4, size, 4 * frames), jnp.float32),
                pltpu.VMEM((4, 2 * cells_z, 2 * frames), jnp.bfloat16),
                pltpu.VMEM((size, 2 * size), jnp.bfloat16),
                pltpu.VMEM((size // 8, size), jnp.float32),
                pltpu.VMEM((size // 8, size), jnp.float32),
            ],
        ),
        out_shape=[
            jax.ShapeDtypeStruct((4, 2 * cells_y, 4 * frames), jnp.bfloat16),
            jax.ShapeDtypeStruct((owners, 16, 4 * frames), jnp.bfloat16),
        ],
        compiler_params=params(),
        cost_estimate=pl.CostEstimate(flops=9_000_000_000, bytes_accessed=14 << 20, transcendentals=0),
        name="first_half",
    )(place, bragg, scales, disp, amp, mask)


def second_kernel(section_ref, rows_ref, out_ref, held):
    step = pl.program_id(0)
    held[step] = dot(rows_ref[0, 0], section_ref[0])

    @pl.when(step == 3)
    def _():
        pack_owners(lambda member, at: held[member, at, :], out_ref, 0)


def second_half(section, rows):
    size = rows.shape[2]
    lanes = section.shape[2]
    owners = size // 4
    return pl.pallas_call(
        second_kernel,
        grid=(4,),
        in_specs=[
            pl.BlockSpec((1, 2 * size, lanes), lambda t: (t, 0, 0)),
            pl.BlockSpec((1, 1, size, 2 * size), lambda t: (t, 1, 0, 0)),
        ],
        out_specs=pl.BlockSpec((owners, 16, lanes), lambda t: (0, 0, 0)),
        out_shape=jax.ShapeDtypeStruct((owners, 16, lanes), jnp.bfloat16),
        scratch_shapes=[pltpu.VMEM((4, size, lanes), jnp.float32)],
        compiler_params=params(),
        cost_estimate=pl.CostEstimate(flops=3_000_000_000, bytes_accessed=10 << 20, transcendentals=0),
        name="second_half",
    )(section, rows)


def middle_kernel(weights_ref, got_ref, counts_ref, cols_ref, rows_ref, *rest):
    out_refs, (wide, far, back, held) = rest[:-4], rest[-4:]
    step = pl.program_id(0)
    owners = got_ref.shape[0]
    size = far.shape[2]
    frames = got_ref.shape[2] // 4
    lanes = 2 * frames

    @pl.when(step == 0)
    def _():
        for group in range(4):
            piece = got_ref[:, :, group * frames : (group + 1) * frames].astype(jnp.float32)
            turned = jnp.swapaxes(piece, 0, 1).astype(jnp.bfloat16)
            for member in range(4):
                for part in range(2):
                    at = (4 * (group // 2) + 2 * part + group % 2) * owners
                    for row in range(2):
                        wide[member, at : at + owners, row * frames : (row + 1) * frames] = turned[
                            4 * member + 2 * part + row
                        ]

    @pl.when(step < 4)
    def _():
        for part in range(2):
            far[step, part] = dot(cols_ref[0, part], wide[step])

    @pl.when(step == 3)
    def _():
        def body(turn, carry):
            at = pl.ds(pl.multiple_of(turn * 16, 16), 16)
            fields = [(far[member, 0, at, :], far[member, 1, at, :]) for member in range(4)]
            intensity = None
            for member, (real, imag) in enumerate(fields):
                term = weights_ref[member] * (real * real + imag * imag)
                intensity = term if intensity is None else intensity + term
            ratio = 1.0 - jnp.sqrt(counts_ref[at, :].astype(jnp.float32) / jnp.maximum(intensity, 0.5))
            for member, (real, imag) in enumerate(fields):
                factor = weights_ref[member] * ratio
                back[member, at, :] = (factor * real).astype(jnp.bfloat16)
                low = pl.ds(pl.multiple_of(size + turn * 16, 16), 16)
                back[member, low, :] = (-factor * imag).astype(jnp.bfloat16)
            return carry

        lax.fori_loop(0, size // 16, body, 0)

    @pl.when(step >= 4)
    def _():
        for half in range(2):
            held[step - 4, half] = dot(rows_ref[0, half], back[step - 4])

    @pl.when(step == 7)
    def _():
        for half in range(2):
            out_ref, place = (out_refs[0], 16 * half) if len(out_refs) == 1 else (out_refs[half], 0)
            pack_owners(lambda member, at, half=half: held[member, half, at, :], out_ref, place)


def middle(weights, got, counts, cols, rows, split):
    owners, _, lanes4 = got.shape
    size = rows.shape[2]
    lanes = lanes4 // 2
    if split:
        shapes = [(owners, 16, lanes)] * 2
    else:
        shapes = [(owners, 32, lanes)]
    return pl.pallas_call(
        middle_kernel,
        grid=(8,),
        in_specs=[
            pl.BlockSpec(memory_space=pltpu.SMEM),
            pl.BlockSpec(got.shape, lambda t: (0, 0, 0)),
            pl.BlockSpec(counts.shape, lambda t: (0, 0)),
            pl.BlockSpec((1, 2, size, 2 * size), lambda t: (jnp.minimum(t, 3), 0, 0, 0)),
            pl.BlockSpec((1, 2, size, 2 * size), lambda t: (jnp.maximum(t - 4, 0), 0, 0, 0)),
        ],
        out_specs=[pl.BlockSpec(shape, lambda t: (0, 0, 0)) for shape in shapes],
        out_shape=[jax.ShapeDtypeStruct(shape, jnp.bfloat16) for shape in shapes],
        scratch_shapes=[
            pltpu.VMEM((4, 2 * size, lanes), jnp.bfloat16),
            pltpu.VMEM((4, 2, size, lanes), jnp.float32),
            pltpu.VMEM((4, 2 * size, lanes), jnp.bfloat16),
            pltpu.VMEM((4, 2, size, lanes), jnp.float32),
        ],
        compiler_params=params(),
        cost_estimate=pl.CostEstimate(flops=9_000_000_000, bytes_accessed=22 << 20, transcendentals=0),
        name="middle",
    )(weights, got, counts, cols, rows)


def turn_rows(got_ref, wide, group, frames, members, first_row, first_lane):
    owners = got_ref.shape[0]
    piece = got_ref[:, first_row : first_row + 16, group * frames : (group + 1) * frames]
    turned = jnp.swapaxes(piece.astype(jnp.float32), 0, 1).astype(jnp.bfloat16)
    for member in range(members):
        for part in range(2):
            at = (2 * part + group) * owners
            for row in range(2):
                lane = first_lane + row * frames
                wide[member, at : at + owners, lane : lane + frames] = turned[4 * member + 2 * part + row]


def early_kernel(got_ref, cols_ref, out_ref, wide):
    member = pl.program_id(0)
    frames = got_ref.shape[2] // 2

    @pl.when(member == 0)
    def _():
        for half in range(2):
            for group in range(2):
                turn_rows(got_ref, wide, group, frames, 4, 16 * half, 2 * half * frames)

    for part in range(2):
        out_ref[0, part] = dot(cols_ref[0, part], wide[member]).astype(jnp.bfloat16)


def early_part(got, cols):
    owners, rows, lanes = got.shape
    size = cols.shape[2]
    return pl.pallas_call(
        early_kernel,
        grid=(4,),
        in_specs=[
            pl.BlockSpec(got.shape, lambda t: (0, 0, 0)),
            pl.BlockSpec((1, 2, size, size), lambda t: (t, 0, 0, 0)),
        ],
        out_specs=pl.BlockSpec((1, 2, size, 2 * lanes), lambda t: (t, 0, 0, 0)),
        out_shape=jax.ShapeDtypeStruct((4, 2, size, 2 * lanes), jnp.bfloat16),
        scratch_shapes=[pltpu.VMEM((4, size, 2 * lanes), jnp.bfloat16)],
        compiler_params=params(),
        cost_estimate=pl.CostEstimate(flops=4_000_000_000, bytes_accessed=10 << 20, transcendentals=0),
        name="early_part",
    )(got, cols)


def last_kernel(
    place_ref, scales_ref, late_ref, real_cols_ref, imag_cols_ref, real_part_ref, imag_part_ref, zb_ref,
    wave_ref, amp_ref, *rest,
):
    out_refs, (wide, field, sum_amp, sum_phase) = rest[:-4], rest[-4:]
    member = pl.program_id(0)
    frames = late_ref.shape[2] // 2
    cells_y, cells_z = amp_ref.shape[1:]

    @pl.when(member == 0)
    def _():
        for group in range(2):
            turn_rows(late_ref, wide, group, frames, 4, 0, 0)
        sum_amp[...] = jnp.zeros_like(sum_amp)
        sum_phase[...] = jnp.zeros_like(sum_phase)

    columns = wide[member]
    real = (dot(real_cols_ref[0, 0], columns) + real_part_ref[0, 0].astype(jnp.float32)).astype(jnp.bfloat16)
    imag = (dot(imag_cols_ref[0, 0], columns) + imag_part_ref[0, 0].astype(jnp.float32)).astype(jnp.bfloat16)
    for row in range(2):
        lane = slice(row * frames, (row + 1) * frames)
        field[row, :, 0:frames] = real[:, lane]
        field[row, :, frames : 2 * frames] = imag[:, lane]
    scale = scales_ref[member]
    tile = 256

    def body(step, carry):
        at = pl.ds(pl.multiple_of(step * tile, tile), tile)
        for row in range(2):
            both = dot(field[row, at, :], zb_ref[0])
            back_real, back_imag = both[:, 0:cells_z], both[:, cells_z : 2 * cells_z]
            wave_real = wave_ref[0, row, at, 0:cells_z].astype(jnp.float32)
            wave_imag = wave_ref[0, row, at, cells_z : 2 * cells_z].astype(jnp.float32)
            sum_amp[row, at, :] += back_real * wave_real - back_imag * wave_imag
            sum_phase[row, at, :] += scale * (back_real * wave_imag + back_imag * wave_real)
        return carry

    lax.fori_loop(0, cells_y // tile, body, 0)

    @pl.when(member == 3)
    def _():
        def close(step, carry):
            at = pl.ds(pl.multiple_of(step * tile, tile), tile)
            for row in range(2):
                out_ref, place = (out_refs[0], row) if len(out_refs) == 1 else (out_refs[row], 0)
                total = sum_amp[row, at, :] / amp_ref[row, at, :].astype(jnp.float32)
                out_ref[place, 0, at, :] = total.astype(jnp.bfloat16)
                out_ref[place, 1, at, :] = sum_phase[row, at, :].astype(jnp.bfloat16)
            return carry

        lax.fori_loop(0, cells_y // tile, close, 0)


def last(place, scales, late, early, cols, zb, wave, amp, half, pieces):
    _, cells_y, cells_z = amp.shape
    owners, _, lanes = late.shape
    size = cols.shape[2]

    def of_part(part, at):
        return lambda t, *_: (t, part, 0, at)

    return pl.pallas_call(
        last_kernel,
        grid_spec=pltpu.PrefetchScalarGridSpec(
            num_scalar_prefetch=2,
            grid=(4,),
            in_specs=[
                pl.BlockSpec((owners, 16, lanes), lambda t, *_: (0, 0, 0)),
                pl.BlockSpec((1, 1, size, size), of_part(0, 1)),
                pl.BlockSpec((1, 1, size, size), of_part(1, 1)),
                pl.BlockSpec((1, 1, size, lanes), of_part(0, half)),
                pl.BlockSpec((1, 1, size, lanes), of_part(1, half)),
                pl.BlockSpec((1,) + zb.shape[1:], lambda t, *_: (t, 0, 0)),
                pl.BlockSpec((1, 2, cells_y, 2 * cells_z), lambda t, *_: (t, half, 0, 0)),
                pl.BlockSpec((2, cells_y, cells_z), lambda t, p, *_: (2 * p[0] + half, 0, 0)),
            ],
            out_specs=[pl.BlockSpec((2 // pieces, 2, cells_y, cells_z), lambda t, *_: (0, 0, 0, 0))] * pieces,
            scratch_shapes=[
                pltpu.VMEM((4, size, lanes), jnp.bfloat16),
                pltpu.VMEM((2, cells_y, lanes), jnp.bfloat16),
                pltpu.VMEM((2, cells_y, cells_z), jnp.float32),
                pltpu.VMEM((2, cells_y, cells_z), jnp.float32),
            ],
        ),
        out_shape=[jax.ShapeDtypeStruct((2 // pieces, 2, cells_y, cells_z), jnp.bfloat16)] * pieces,
        compiler_params=params(),
        cost_estimate=pl.CostEstimate(flops=4_000_000_000, bytes_accessed=16 << 20, transcendentals=0),
        name="last",
    )(place, scales, late, cols, cols, early, early, zb, wave, amp)


def finish_kernel(place_ref, bragg_ref, sums_ref, amp_ref, disp_ref, *rest):
    new_amp_ref, new_disp_ref = rest[-2:]
    new_amp_ref[0] = amp_ref[0].astype(jnp.float32) - step_size * sums_ref[0, 0].astype(jnp.float32)
    sum_phase = sums_ref[0, 1].astype(jnp.float32)
    for axis in range(3):
        new_disp_ref[axis, 0] = (
            disp_ref[axis, 0].astype(jnp.float32) + (step_size * bragg_ref[axis]) * sum_phase
        ).astype(jnp.bfloat16)


def finish(place, bragg, sums, amp, disp, earlier, first_row, other):
    rows = sums.shape[0]
    _, cells_y, cells_z = amp.shape

    def row(t, p):
        half = 1 - p[0] if other else p[0]
        return 4 * half + first_row + t

    amp_spec = pl.BlockSpec((1, cells_y, cells_z), lambda t, p, *_: (row(t, p), 0, 0))
    disp_spec = pl.BlockSpec((3, 1, cells_y, cells_z), lambda t, p, *_: (0, row(t, p), 0, 0))
    kept = [] if earlier is None else list(earlier)
    return pl.pallas_call(
        finish_kernel,
        grid_spec=pltpu.PrefetchScalarGridSpec(
            num_scalar_prefetch=2,
            grid=(rows,),
            in_specs=[
                pl.BlockSpec((1, 2, cells_y, cells_z), lambda t, *_: (t, 0, 0, 0)),
                amp_spec,
                disp_spec,
            ]
            + [pl.BlockSpec(memory_space=pl.ANY)] * len(kept),
            out_specs=[amp_spec, disp_spec],
        ),
        out_shape=[
            jax.ShapeDtypeStruct(amp.shape, jnp.float32),
            jax.ShapeDtypeStruct(disp.shape, jnp.bfloat16),
        ],
        input_output_aliases={} if earlier is None else {5: 0, 6: 1},
        compiler_params=params(small_limit),
        cost_estimate=pl.CostEstimate(flops=10_000_000, bytes_accessed=(3 << 20) * rows, transcendentals=0),
        name="finish",
    )(place, bragg, sums, amp, disp, *kept)


def exchange(blocks):
    return lax.all_to_all(blocks, both_axes, split_axis=0, concat_axis=0, tiled=True)


def swap(values):
    return lax.ppermute(values, "spec", [(0, 1), (1, 0)])


def nothing(*refs):
    pass


def after(values, *others):
    anywhere = pl.BlockSpec(memory_space=pl.ANY)
    return pl.pallas_call(
        nothing,
        in_specs=[anywhere] * (1 + len(others)),
        out_specs=anywhere,
        out_shape=jax.ShapeDtypeStruct(values.shape, values.dtype),
        input_output_aliases={0: 0},
        compiler_params=params(),
        name="after",
    )(values, *others)


def per_device(amplitude, displacement, support, counts, bin_weights, bin_scales, bragg_vector):
    place = lax.axis_index("spec").reshape(1).astype(jnp.int32)
    size, rows_y, frames = counts.shape
    cells_z = amplitude.shape[2]
    volume = (place, bragg_vector, bin_scales, displacement, amplitude, support)
    section, blocks = first_half(*volume, size, frames)
    sent_early = exchange(blocks)
    rows = row_matrices(bin_scales, size)
    wave = waves(*volume)
    sent_late = exchange(after(second_half(section, rows), sent_early, wave))
    cols, zb = column_matrices(bin_scales, size, cells_z, frames)
    mine = lax.dynamic_slice_in_dim(counts, place[0] * (rows_y // 2), rows_y // 2, axis=1)
    mine = mine.reshape(size, rows_y // 2 * frames)
    early_counts, late_counts = mine[:, 0 : 2 * frames], mine[:, 2 * frames : 4 * frames]
    (early,) = middle(bin_weights, sent_early, early_counts, cols, rows, False)
    early = exchange(after(early, sent_late))
    parts = middle(bin_weights, sent_late, late_counts, cols, rows, True)
    early_sum = early_part(early, cols)
    late = [exchange(after(parts[0], early))]
    late.append(exchange(after(parts[1], early_sum, late[0])))
    sums = []
    for half in range(2):
        parts = last(
            place, bin_scales, late[half], early_sum, cols, zb, wave, amplitude, half, 1 + half
        )
        for number, part in enumerate(parts):
            sums.append((2 * half + number, part, swap(part)))
    outs = None
    for other in (False, True):
        for row, mine, theirs in sums:
            outs = finish(
                place, bragg_vector, theirs if other else mine, amplitude, displacement, outs, row, other
            )
    return tuple(outs)


def solution(mesh):
    in_specs = (
        P("slab", None, None),
        P(None, "slab", None, None),
        P("slab", None, None),
        P(None, "slab", None),
        P(),
        P(),
        P(),
    )
    out_specs = (P("slab", None, None), P(None, "slab", None, None))
    return jax.shard_map(
        per_device, mesh=mesh, in_specs=in_specs, out_specs=out_specs, check_vma=False
    )
```
